768 devices in a mesh: blk: 64 (over z_lo, y, core), grp: 12 (over z_hi, x).
Axes of the slice: x: 4, y: 8, z: 12 (z_hi: 3, z_lo: 4; z = z_hi * 4 + z_lo), core: 2. Of those that a mesh axis runs over, the one named last changes fastest.
Arguments:
- user_embed: float32 [98304, 256], P(('blk', 'grp')), may hold values from -6 to 6
- item_embed: float32 [12, 4096, 256], P('grp', 'blk'), may hold values from -6 to 6
- user_degree: int32 [98304], P(('blk', 'grp')), may hold values from 1 to 99
- item_degree: int32 [12, 4096], P('grp', 'blk'), may hold values from 1 to 99
- tile_values: bfloat16 [2048, 24, 128, 128], P('blk', 'grp'), may hold values from 0.049804688 to 1
- tile_rows: int32 [2048, 24], P('blk', 'grp'), may hold values from 0 to 12, as said below
Outputs:
- user_out: float32 [98304, 256], P(('blk', 'grp'))
- item_out: float32 [12, 4096, 256], P('grp', 'blk')
The draws below stay inside these ranges and needn't reach their ends.
Inputs may be any that keep to these rules, and one draw needn't show every extreme that they name: `tile_rows`: within one column block of one device the live slots name different row blocks, the first slot is always live, and a slot that holds 12 is empty.
All inputs are finite; a program needn't handle non-finite values.
Results may differ from the reference program's by a relative error of at most 0.0027.
Values may be sent and summed in bfloat16 or wider, within the bound.
A program may use at most 64 MiB of HBM per device.

```python
import math
import jax
import jax.numpy as jnp
from jax import lax

D = 256
TILE = 128
SLOTS = 2
COL_BLOCKS = 32
COL_ITEMS = 4096
USERS = 98304
N_BLK = 64
N_GRP = 12


def draw_tile_rows(key, part):
    key = jax.random.fold_in(key, 7)
    key_level = jax.random.fold_in(key, 1)
    key_count = jax.random.fold_in(key, 2)
    key_order = jax.random.fold_in(key, 3)
    level = jax.random.randint(key_level, (N_BLK, 1, N_GRP, 1), 1, SLOTS + 1)
    count = jax.random.randint(key_count, (N_BLK, COL_BLOCKS, N_GRP, 1), 0, 1 << 20) % level + 1
    count = count.at[0, 0, 0, 0].set(1)
    scores = jax.random.randint(key_order, (N_BLK, COL_BLOCKS, N_GRP, N_GRP), 0, 1 << 16) * N_GRP + jnp.arange(N_GRP, dtype=jnp.int32)
    order = jnp.argsort(scores, axis=-1)[..., :SLOTS].astype(jnp.int32)
    slot_index = jnp.arange(SLOTS, dtype=jnp.int32)
    rows = jnp.where(slot_index < count, order, N_GRP)
    return rows.reshape(N_BLK * COL_BLOCKS, N_GRP * SLOTS).astype(jnp.int32)


def place_ends(result, rng, low, top_value):
    place = [jax.random.randint(jax.random.fold_in(rng, axis), (), 0, length) for axis, length in enumerate(result.shape)]
    longest = result.shape.index(max(result.shape))
    neighbour = place[:longest] + [(place[longest] + 1) % result.shape[longest]] + place[longest + 1:]
    return result.at[tuple(place)].set(low).at[tuple(neighbour)].set(top_value)


def block_scale(own_key, dims, pieces, low, high):
    def one(position, parts):
        draws = jax.random.uniform(jax.random.fold_in(jax.random.fold_in(own_key, 6), position), (parts,), jnp.float32, low / len(pieces), high / len(pieces))
        return jnp.repeat(jnp.exp(draws), dims[position] // parts).reshape((-1,) + (1,) * (len(dims) - position - 1))

    level = one(*pieces[0])
    for cut in pieces[1:]:
        level = level * one(*cut)
    return level


def gaussian(stream_key, extent, width, reach, split=(), kind=jnp.bfloat16):
    result = width * jax.random.normal(stream_key, extent, jnp.float32)
    if split:
        result = result * block_scale(stream_key, extent, split, -0.22, 0.18)
    return jnp.clip(result, -reach, reach).astype(kind)


def setup_inputs(seed: int = 0) -> dict:
    arg_keys = jax.random.split(jax.random.key(seed), 7)
    return {
        "user_embed": gaussian(arg_keys[0], (USERS, D), 1.0, 6.0, ((0, 768),), jnp.float32),
        "item_embed": gaussian(arg_keys[1], (N_GRP, COL_ITEMS, D), 1.0, 6.0, ((0, 12), (1, 64)), jnp.float32),
        "user_degree": place_ends(jax.random.randint(arg_keys[2], (USERS,), 1, 100), jax.random.fold_in(arg_keys[2], 1), 1, 99).astype(jnp.int32),
        "item_degree": place_ends(jax.random.randint(arg_keys[3], (N_GRP, COL_ITEMS), 1, 100), jax.random.fold_in(arg_keys[3], 1), 1, 99).astype(jnp.int32),
        "tile_values": jnp.clip(jnp.exp(math.log(1.0) - 2.9996462 * jax.random.uniform(arg_keys[4], (N_BLK * COL_BLOCKS, N_GRP * SLOTS, TILE, TILE), jnp.float32) ** block_scale(arg_keys[4], (N_BLK * COL_BLOCKS, N_GRP * SLOTS, TILE, TILE), ((0, 64), (1, 12)), -0.2, 0.2)), 0.049804688, 1.0).astype(jnp.bfloat16),
        "tile_rows": draw_tile_rows(jax.random.fold_in(arg_keys[6], 71), 0),
    }


def reference(user_embed, item_embed, user_degree, item_degree, tile_values, tile_rows):
    scaled_items = (item_embed * lax.rsqrt(item_degree.astype(jnp.float32))[..., None]).astype(jnp.bfloat16)
    scaled_users = (user_embed * lax.rsqrt(user_degree.astype(jnp.float32))[:, None]).astype(jnp.bfloat16)
    tiles = tile_values.reshape(N_BLK, COL_BLOCKS, N_GRP, SLOTS, TILE, TILE)
    rows = tile_rows.reshape(N_BLK, COL_BLOCKS, N_GRP, SLOTS)
    item_blocks = scaled_items.reshape(N_GRP, COL_BLOCKS, TILE, D).astype(jnp.float32)
    user_blocks = scaled_users.reshape(N_BLK, N_GRP, TILE, D)

    def step(carry, inputs):
        tile_block, row_block, user_block = inputs
        tile_float = tile_block.astype(jnp.float32)
        row_onehot = (row_block[..., None] == jnp.arange(N_GRP, dtype=jnp.int32)).astype(jnp.float32)
        products = jnp.einsum('cgstj,gcjd->cgstd', tile_float, item_blocks)
        forward = jnp.einsum('cgsr,cgstd->rtd', row_onehot, products)
        padded = jnp.concatenate([user_block, jnp.zeros((1, TILE, D), jnp.bfloat16)], 0).astype(jnp.float32)
        selected = padded[row_block]
        backward = jnp.einsum('cgstj,cgstd->gcjd', tile_float, selected)
        return (carry + backward, forward)
    start = jnp.zeros((N_GRP, COL_BLOCKS, TILE, D), jnp.float32)
    item_sums, user_sums = lax.scan(step, start, (tiles, rows, user_blocks))
    user_sums = user_sums.reshape(USERS, D)
    item_sums = item_sums.reshape(N_GRP, COL_ITEMS, D)
    user_out = 0.5 * (user_embed + lax.rsqrt(user_degree.astype(jnp.float32))[:, None] * user_sums)
    item_out = 0.5 * (item_embed + lax.rsqrt(item_degree.astype(jnp.float32))[..., None] * item_sums)
    return (user_out, item_out)
```

```python
import jax
import jax.numpy as jnp
from jax import lax
from jax.experimental import pallas as pl
from jax.experimental.pallas import tpu as pltpu
from jax.sharding import PartitionSpec as P

NZ, NY, NC = 4, 8, 2
NH, NX = 3, 4
TILE = 128
HALF = 64
D = 256
COLS = NZ * NY
SLOTS = 2
NT = COLS * SLOTS
ROWS = NH * NX
F32, BF16 = jnp.float32, jnp.bfloat16
MESH = pl.DeviceIdType.MESH
GROUPS = (4, 3, -3, 2, -2, 1, -1, 0)


def valid_gather(d, s, p):
    return s <= 2 or (s == 3 and p == d)


def column(row):
    n = row.shape[1]
    a = lax.broadcasted_iota(jnp.int32, (n, n), 0)
    b = lax.broadcasted_iota(jnp.int32, (n, n), 1)
    return jnp.sum(jnp.where(a == b, jnp.broadcast_to(row, (n, n)), 0.0), axis=1, keepdims=True)


def kernel(
    ue, ie, ud, ideg, tv, rows, uo, io,
    X, U, T, TT, S, PS, R, SB, RB, ZS, ZR, VS0, VR0, VS1, VR1, US, UR, keys, plan, order,
    tsem, osem, send, xz, xy, xs, uz, ux, uh, ps, ry, rz, v0, v1, vz,
):
    b = lax.axis_index("blk")
    g = lax.axis_index("grp")
    core = b % 2
    y = (b // 2) % NY
    zl = b // (2 * NY)
    x = g % NX
    zh = g // NX
    other = 1 - core

    def blk(z_, y_, c_):
        return {"blk": (z_ * NY + y_) * NC + c_}

    def grp(h_, x_):
        return {"grp": h_ * NX + x_}

    sib = blk(zl, y, other)
    ydev = (blk(zl, (y + 1) % NY, core), blk(zl, (y + NY - 1) % NY, core))
    zrel = (zl, zl + 1 - 2 * (zl % 2), (zl + 2) % NZ, NZ - 1 - zl)
    zdev = tuple(blk(z_, y, core) for z_ in zrel)
    xdev = (grp(zh, (x + 1) % NX), grp(zh, (x + NX - 1) % NX))
    hrel = (zh, (zh + NH - 1) % NH, (zh + 1) % NH)
    hdev = (None, grp(hrel[1], x), grp(hrel[2], x))
    pb0 = (zl // 2) * 2
    pb = (pb0, 2 - pb0)

    bar = pltpu.get_barrier_semaphore()
    peers = (sib,) + ydev + zdev[1:] + xdev + hdev[1:]
    for dev in peers:
        pl.semaphore_signal(bar, inc=1, device_id=dev, device_id_type=MESH)

    tcopy = pltpu.make_async_copy(tv, T, tsem)
    tcopy.start()

    sends = []

    def put(src, dst, rsem, dev):
        c = pltpu.make_async_remote_copy(
            src_ref=src, dst_ref=dst, send_sem=send.at[len(sends)], recv_sem=rsem,
            device_id=dev, device_id_type=MESH,
        )
        c.start()
        sends.append(c)

    def got(dst, rsem, dev):
        pltpu.make_async_remote_copy(
            src_ref=dst, dst_ref=dst, send_sem=send.at[0], recv_sem=rsem,
            device_id=dev, device_id_type=MESH,
        ).wait_recv()

    iscale = column(lax.rsqrt(ideg[...].astype(F32)))
    uscale = column(lax.rsqrt(ud[...].astype(F32)))
    X[y * NZ + zl, core] = (ie[...] * iscale).astype(BF16)
    U[g] = (ue[...] * uscale).astype(BF16)
    U[ROWS] = jnp.zeros((TILE, D), BF16)

    pl.semaphore_wait(bar, len(peers))

    own = X.at[y * NZ + zl, core]
    for k in (1, 3, 2):
        put(own, own, xz.at[k - 1], zdev[k])
    for j in (1, 2):
        put(U.at[g], U.at[g], uz.at[2 - j], hdev[j])
    for d in (0, 1):
        put(U.at[g], U.at[g], ux.at[d, 0], xdev[d])

    def xreg(yy, p, c):
        return X.at[pl.ds(yy * NZ + pb[p], 2), c]

    def yfrom(d, s):
        return (y + NY - 1 - s) % NY if d == 0 else (y + 1 + s) % NY

    for i in range(NT):
        keys[i : i + 1, :] = jnp.full((1, 128), rows[i // SLOTS, i % SLOTS], jnp.int32)
    kc = keys[...]
    sub = lax.broadcasted_iota(jnp.int32, (NT, 128), 0)
    lane = lax.broadcasted_iota(jnp.int32, (NT, 128), 1)
    uc = kc * NT + sub
    ur = jnp.sum(jnp.where(sub == lane, uc, 0), axis=0, keepdims=True)
    ur = jnp.where(lax.broadcasted_iota(jnp.int32, (1, 128), 1) < NT, ur, 1 << 20)
    rank = jnp.sum(jnp.where(ur < uc, 1, 0), axis=1, keepdims=True)
    hit = rank == lane
    plan[...] = jnp.zeros((8, 128), jnp.int32)
    plan[0:1, :] = jnp.sum(jnp.where(hit, sub, 0), axis=0, keepdims=True)
    plan[1:2, :] = jnp.sum(jnp.where(hit, kc, 0), axis=0, keepdims=True)
    upto = jnp.sum(jnp.where(kc <= lane, 1, 0), axis=0, keepdims=True)
    count = jnp.sum(jnp.where(kc == lane, 1, 0), axis=0, keepdims=True)
    plan[2:3, :] = jnp.where(count > 0, upto, 0)
    ocopy = pltpu.make_async_copy(plan, order, osem)
    ocopy.start()

    def xfirst(p):
        for d in (0, 1):
            put(xreg(y, p, core), xreg(y, p, core), xy.at[d, 0, p], ydev[d])

    def zgot(k):
        r = X.at[y * NZ + zrel[k], core]
        got(r, xz.at[k - 1], zdev[k])

    zgot(1)
    xfirst(0)
    zgot(3)
    zgot(2)
    xfirst(1)
    r = X.at[pl.ds(y * NZ, NZ), core]
    put(r, r, xs.at[0, 4, 0], sib)

    tcopy.wait()

    def flip(c, _):
        TT[c, :, 0:TILE] = T[2 * c].T
        TT[c, :, TILE:] = T[2 * c + 1].T
        return 0

    lax.fori_loop(0, COLS, flip, 0)

    def uslot(j, x_):
        return hrel[j] * NX + x_

    xnb = ((x + NX - 1) % NX, (x + 1) % NX)

    def users_pass(j):
        for d in (0, 1):
            s = uslot(j, xnb[d])
            got(U.at[s], ux.at[d, j], xdev[1 - d])
            h = U.at[s, pl.ds(d * HALF, HALF)]
            put(h, h, uh.at[d, j], xdev[d])

    def users_far(j):
        s = uslot(j, (x + 2) % NX)
        for d in (0, 1):
            got(U.at[s, pl.ds(d * HALF, HALF)], uh.at[d, j], xdev[1 - d])

    def items_pass(s):
        for p in (0, 1):
            for d in (0, 1):
                if not valid_gather(d, s, p):
                    continue
                yy = yfrom(d, s)
                r = xreg(yy, p, core)
                got(r, xy.at[d, s, p], ydev[1 - d])
                if valid_gather(d, s + 1, p):
                    put(r, r, xy.at[d, s + 1, p], ydev[d])
                put(r, r, xs.at[d, s, p], sib)

    users_pass(0)
    items_pass(0)
    for j in (1, 2):
        s = uslot(j, x)
        got(U.at[s], uz.at[j - 1], hdev[j])
        for d in (0, 1):
            put(U.at[s], U.at[s], ux.at[d, j], xdev[d])
    items_pass(1)
    users_pass(1)
    users_pass(2)
    items_pass(2)
    for j in (0, 1, 2):
        users_far(j)

    for i, off in enumerate(GROUPS):
        yd = (y + NY + off) % NY

        def one(z_, _, yd=yd):
            c = z_ * NY + yd
            lhs = TT[c]
            rhs = jnp.concatenate([U[rows[c, 0]], U[rows[c, 1]]], axis=0)
            out = jnp.dot(lhs, rhs, preferred_element_type=F32)
            PS[yd * NZ + z_] = out.reshape(NC, HALF, D)
            return 0

        lax.fori_loop(0, NZ, one, 0)
        put(PS.at[pl.ds(yd * NZ, NZ), other], R.at[pl.ds(yd * NZ, NZ)], ps.at[i], sib)

    items_pass(3)

    def pgot(i):
        yd = (y + NY + GROUPS[i]) % NY
        got(R.at[pl.ds(yd * NZ, NZ)], ps.at[i], sib)

    def sum_step(d, s, p):
        yd = (y + 4 - s) % NY if d == 0 else (y + NY - 4 + s) % NY
        q = pl.ds(yd * NZ + pb[p], 2)
        val = PS[q, core] + R[q]
        if not (s == 0 or (s == 1 and p != d)):
            got(RB.at[d, s - 1, p], ry.at[d, s - 1, p], ydev[1 - d])
            val = val + RB[d, s - 1, p].astype(F32)
        SB[d, s, p] = val.astype(BF16)
        put(SB.at[d, s, p], RB.at[d, s, p], ry.at[d, s, p], ydev[d])

    pgot(0)
    sum_step(0, 0, 0)
    sum_step(1, 0, 1)
    pgot(1)
    pgot(2)
    sum_step(0, 1, 1)
    sum_step(1, 1, 0)

    r = X.at[pl.ds(y * NZ, NZ), other]
    got(r, xs.at[0, 4, 0], sib)
    for s in range(4):
        for p in (0, 1):
            for d in (0, 1):
                if valid_gather(d, s, p):
                    got(xreg(yfrom(d, s), p, other), xs.at[d, s, p], sib)
    ocopy.wait()

    S[0] = jnp.zeros((TILE, D), F32)

    def forward(k, _):
        o = order[0, k]
        c = o // SLOTS
        keep = jnp.where(order[1, k] == order[1, jnp.maximum(k - 1, 0)], 1.0, 0.0)
        xb = X[(c % NY) * NZ + c // NY].reshape(TILE, D)
        S[k + 1] = S[k] * keep + jnp.dot(T[o], xb, preferred_element_type=F32)
        return 0

    lax.fori_loop(0, NT // 2, forward, 0)
    sum_step(0, 1, 0)
    sum_step(1, 1, 1)
    lax.fori_loop(NT // 2, NT, forward, 0)

    def user_sum(h_, x_):
        return S[order[2, h_ * NX + x_]]

    for h in range(NH):
        v = user_sum(h, (x + 2) % NX).astype(BF16)
        for d in (0, 1):
            VS0[d, h] = v[d * HALF : (d + 1) * HALF]
    for d in (0, 1):
        put(VS0.at[d], VR0.at[d], v0.at[d], xdev[d])

    pgot(3)
    pgot(4)
    for p in (0, 1):
        for d in (0, 1):
            sum_step(d, 2, p)

    for d in (0, 1):
        got(VR0.at[d], v0.at[d], xdev[1 - d])
        for h in range(NH):
            v = user_sum(h, (x + 1) % NX if d == 0 else (x + NX - 1) % NX)
            f = VR0[d, h].astype(F32)
            lo, hi = v[:HALF], v[HALF:]
            lo, hi = (lo + f, hi) if d == 0 else (lo, hi + f)
            VS1[d, h, :HALF] = lo.astype(BF16)
            VS1[d, h, HALF:] = hi.astype(BF16)
        put(VS1.at[d], VR1.at[d], v1.at[d], xdev[d])

    pgot(5)
    pgot(6)
    for p in (0, 1):
        for d in (0, 1):
            sum_step(d, 3, p)

    for d in (0, 1):
        got(VR1.at[d], v1.at[d], xdev[1 - d])

    def user_total(h_):
        return user_sum(h_, x) + VR1[0, h_].astype(F32) + VR1[1, h_].astype(F32)

    for j in (1, 2):
        US[j - 1] = user_total(hrel[j]).astype(BF16)
        put(US.at[j - 1], UR.at[2 - j], vz.at[2 - j], hdev[j])

    pgot(7)
    for p in (0, 1):
        for d in (0, 1):
            got(RB.at[d, 3, p], ry.at[d, 3, p], ydev[1 - d])
        q = pl.ds(y * NZ + pb[p], 2)
        ZS[pl.ds(pb[p], 2)] = (
            PS[q, core] + R[q] + RB[0, 3, p].astype(F32) + RB[1, 3, p].astype(F32)
        )
        if p == 0:
            put(ZS.at[zrel[1]], ZR.at[0], rz.at[0], zdev[1])
    for k in (2, 3):
        put(ZS.at[zrel[k]], ZR.at[k - 1], rz.at[k - 1], zdev[k])

    total = user_total(zh)
    for j in (1, 2):
        got(UR.at[j - 1], vz.at[j - 1], hdev[j])
        total = total + UR[j - 1].astype(F32)
    uo[...] = 0.5 * (ue[...] + uscale * total)

    acc = ZS[zl]
    for k in (1, 2, 3):
        got(ZR.at[k - 1], rz.at[k - 1], zdev[k])
        acc = acc + ZR[k - 1]
    io[...] = 0.5 * (ie[...] + iscale * acc)

    for c in sends:
        c.wait_send()


def on_device(user_embed, item_embed, user_degree, item_degree, tile_values, tile_rows):
    vm = pl.BlockSpec(memory_space=pltpu.VMEM)
    dma = pltpu.SemaphoreType.DMA
    user_out, item_out = pl.pallas_call(
        kernel,
        out_shape=(
            jax.ShapeDtypeStruct((TILE, D), F32),
            jax.ShapeDtypeStruct((HALF, D), F32),
        ),
        in_specs=[vm, vm, vm, vm, pl.BlockSpec(memory_space=pl.ANY), pl.BlockSpec(memory_space=pltpu.SMEM)],
        out_specs=(vm, vm),
        scratch_shapes=[
            pltpu.VMEM((COLS, NC, HALF, D), BF16),
            pltpu.VMEM((ROWS + 1, TILE, D), BF16),
            pltpu.VMEM((NT, TILE, TILE), BF16),
            pltpu.VMEM((COLS, TILE, SLOTS * TILE), BF16),
            pltpu.VMEM((NT + 1, TILE, D), F32),
            pltpu.VMEM((COLS, NC, HALF, D), F32),
            pltpu.VMEM((COLS, HALF, D), F32),
            pltpu.VMEM((2, 4, 2, 2, HALF, D), BF16),
            pltpu.VMEM((2, 4, 2, 2, HALF, D), BF16),
            pltpu.VMEM((NZ, HALF, D), F32),
            pltpu.VMEM((NZ - 1, HALF, D), F32),
            pltpu.VMEM((2, NH, HALF, D), BF16),
            pltpu.VMEM((2, NH, HALF, D), BF16),
            pltpu.VMEM((2, NH, TILE, D), BF16),
            pltpu.VMEM((2, NH, TILE, D), BF16),
            pltpu.VMEM((2, TILE, D), BF16),
            pltpu.VMEM((2, TILE, D), BF16),
            pltpu.VMEM((NT, 128), jnp.int32),
            pltpu.VMEM((8, 128), jnp.int32),
            pltpu.SMEM((8, 128), jnp.int32),
            dma(()),
            dma(()),
            dma((96,)),
            dma((3,)),
            dma((2, 4, 2)),
            dma((2, 5, 2)),
            dma((2,)),
            dma((2, 3)),
            dma((2, 3)),
            dma((8,)),
            dma((2, 4, 2)),
            dma((3,)),
            dma((2,)),
            dma((2,)),
            dma((2,)),
        ],
        compiler_params=pltpu.CompilerParams(
            collective_id=0, has_side_effects=True, vmem_limit_bytes=48 << 20
        ),
    )(
        user_embed,
        item_embed[0],
        user_degree.reshape(1, TILE),
        item_degree,
        tile_values.reshape(NT, TILE, TILE),
        tile_rows,
    )
    return user_out, item_out[None]


def solution(mesh):
    return jax.shard_map(
        on_device,
        mesh=mesh,
        in_specs=(
            P(("blk", "grp"), None),
            P("grp", "blk", None),
            P(("blk", "grp")),
            P("grp", "blk"),
            P("blk", "grp", None, None),
            P("blk", "grp"),
        ),
        out_specs=(P(("blk", "grp"), None), P("grp", "blk", None)),
        check_vma=False,
    )
```

```python
import jax
import jax.numpy as jnp
from jax import lax
from jax.experimental import pallas as pl
from jax.experimental.pallas import tpu as pltpu
from jax.sharding import PartitionSpec as P

NZ, NY, NC = 4, 8, 2
NH, NX = 3, 4
TILE = 128
HALF = 64
D = 256
COLS = NZ * NY
SLOTS = 2
NT = COLS * SLOTS
ROWS = NH * NX
F32, BF16 = jnp.float32, jnp.bfloat16
MESH = pl.DeviceIdType.MESH
GROUPS = (4, 3, -3, 2, -2, 1, -1, 0)


def valid_gather(d, s, p):
    return s <= 2 or (s == 3 and p == d)


def column(row):
    n = row.shape[1]
    a = lax.broadcasted_iota(jnp.int32, (n, n), 0)
    b = lax.broadcasted_iota(jnp.int32, (n, n), 1)
    return jnp.sum(jnp.where(a == b, jnp.broadcast_to(row, (n, n)), 0.0), axis=1, keepdims=True)


def kernel(
    ue_h, ie_h, ud_h, ideg_h, tv, rows_h, uo, io,
    X, U, T, TT, Q, S, PS, R, SB, RB, ZS, ZR, VS, VR, US, UR, keys, plan, ue, ie, ud, ideg, order, rows,
    isem, osem, send, xz, xy, xs, uz, ux, ps, ry, rz, v0, vz,
):
    b = lax.axis_index("blk")
    g = lax.axis_index("grp")
    core = b % 2
    y = (b // 2) % NY
    zl = b // (2 * NY)
    x = g % NX
    zh = g // NX
    other = 1 - core

    def blk(z_, y_, c_):
        return {"blk": (z_ * NY + y_) * NC + c_}

    def grp(h_, x_):
        return {"grp": h_ * NX + x_}

    sib = blk(zl, y, other)
    ydev = (blk(zl, (y + 1) % NY, core), blk(zl, (y + NY - 1) % NY, core))
    zrel = (zl, zl + 1 - 2 * (zl % 2), (zl + 2) % NZ, NZ - 1 - zl)
    zdev = tuple(blk(z_, y, core) for z_ in zrel)
    xrel = tuple((x + e) % NX for e in range(NX))
    xdev = tuple(grp(zh, x_) for x_ in xrel)
    hrel = (zh, (zh + NH - 1) % NH, (zh + 1) % NH)
    hdev = (None, grp(hrel[1], x), grp(hrel[2], x))
    pb0 = (zl // 2) * 2
    pb = (pb0, 2 - pb0)

    bar = pltpu.get_barrier_semaphore()
    peers = (sib,) + ydev + zdev[1:] + xdev[1:] + hdev[1:]
    for dev in peers:
        pl.semaphore_signal(bar, inc=1, device_id=dev, device_id_type=MESH)

    fetch = [
        pltpu.make_async_copy(a, v, isem.at[n])
        for n, (a, v) in enumerate(
            ((ideg_h, ideg), (ud_h, ud), (ie_h, ie), (ue_h, ue), (rows_h, rows), (tv, T))
        )
    ]
    for c in fetch:
        c.start()

    sends = []

    def put(src, dst, rsem, dev):
        c = pltpu.make_async_remote_copy(
            src_ref=src, dst_ref=dst, send_sem=send.at[len(sends)], recv_sem=rsem,
            device_id=dev, device_id_type=MESH,
        )
        c.start()
        sends.append(c)

    def got(dst, rsem, dev):
        pltpu.make_async_remote_copy(
            src_ref=dst, dst_ref=dst, send_sem=send.at[0], recv_sem=rsem,
            device_id=dev, device_id_type=MESH,
        ).wait_recv()

    for c in fetch[:4]:
        c.wait()
    iscale = column(lax.rsqrt(ideg[...].astype(F32)))
    uscale = column(lax.rsqrt(ud[...].astype(F32)))
    X[y * NZ + zl, core] = (ie[...] * iscale).astype(BF16)
    U[g] = (ue[...] * uscale).astype(BF16)
    U[ROWS] = jnp.zeros((TILE, D), BF16)

    pl.semaphore_wait(bar, len(peers))

    own = X.at[y * NZ + zl, core]
    for k in (1, 3, 2):
        put(own, own, xz.at[k - 1], zdev[k])
    for j in (1, 2):
        put(U.at[g], U.at[g], uz.at[2 - j], hdev[j])

    def users_x(j):
        s = U.at[hrel[j] * NX + x]
        for e in (2, 1, 3):
            put(s, s, ux.at[e - 1, j], xdev[e])

    users_x(0)

    def xreg(yy, p, c):
        return X.at[pl.ds(yy * NZ + pb[p], 2), c]

    def yfrom(d, s):
        return (y + NY - 1 - s) % NY if d == 0 else (y + 1 + s) % NY

    fetch[4].wait()
    for i in range(NT):
        keys[i : i + 1, :] = jnp.full((1, 128), rows[i % SLOTS, i // SLOTS], jnp.int32)
    sub = lax.broadcasted_iota(jnp.int32, (NT, 128), 0)
    lane = lax.broadcasted_iota(jnp.int32, (NT, 128), 1)
    late = (sub // SLOTS) % NY == (y + 4) % NY
    kc = keys[...]
    kl = jnp.where(late, kc + 16, kc)
    uc = kl * NT + sub
    ur = jnp.sum(jnp.where(sub == lane, uc, 0), axis=0, keepdims=True)
    ur = jnp.where(lax.broadcasted_iota(jnp.int32, (1, 128), 1) < NT, ur, 1 << 20)
    rank = jnp.sum(jnp.where(ur < uc, 1, 0), axis=1, keepdims=True)
    hit = rank == lane

    def total(m, v):
        return jnp.sum(jnp.where(m, v, 0), axis=0, keepdims=True)

    plan[...] = jnp.zeros((8, 128), jnp.int32)
    plan[0:1, :] = total(hit, sub)
    plan[1:2, :] = total(hit, kl)
    plan[2:3, :] = jnp.where(total(kl == lane, 1) > 0, total(kl <= lane, 1), 0)
    plan[3:4, :] = jnp.where(total(kl == lane + 16, 1) > 0, total(kl <= lane + 16, 1), 0)
    ocopy = pltpu.make_async_copy(plan, order, osem)
    ocopy.start()

    def xfirst(p):
        for d in (0, 1):
            put(xreg(y, p, core), xreg(y, p, core), xy.at[d, 0, p], ydev[d])

    def zgot(k):
        r = X.at[y * NZ + zrel[k], core]
        got(r, xz.at[k - 1], zdev[k])

    def flip(c, _):
        TT[c, :, 0:TILE] = T[2 * c].T
        TT[c, :, TILE:] = T[2 * c + 1].T
        return 0

    def flips(lo, hi):
        lax.fori_loop(lo, hi, flip, 0, unroll=2)

    def items_pass(s, p):
        for d in (0, 1):
            if not valid_gather(d, s, p):
                continue
            yy = yfrom(d, s)
            r = xreg(yy, p, core)
            got(r, xy.at[d, s, p], ydev[1 - d])
            if valid_gather(d, s + 1, p):
                put(r, r, xy.at[d, s + 1, p], ydev[d])
            put(r, r, xs.at[d, s, p], sib)

    def items_sib(s):
        for p in (0, 1):
            for d in (0, 1):
                if valid_gather(d, s, p):
                    got(xreg(yfrom(d, s), p, other), xs.at[d, s, p], sib)

    def products(yy):
        def one(z_, _):
            c = z_ * NY + yy
            lhs = T[pl.ds(2 * c, 2)].reshape(SLOTS * TILE, TILE)
            out = jnp.dot(lhs, X[yy * NZ + z_].reshape(TILE, D), preferred_element_type=F32)
            Q[pl.ds(2 * c, 2)] = out.reshape(SLOTS, TILE, D)
            return 0

        lax.fori_loop(0, NZ, one, 0, unroll=2)

    def partial(i):
        yd = (y + NY + GROUPS[i]) % NY

        def one(z_, _):
            c = z_ * NY + yd
            rhs = jnp.concatenate([U[rows[0, c]], U[rows[1, c]]], axis=0)
            out = jnp.dot(TT[c], rhs, preferred_element_type=F32)
            PS[yd * NZ + z_] = out.reshape(NC, HALF, D)
            return 0

        lax.fori_loop(0, NZ, one, 0, unroll=2)
        put(PS.at[pl.ds(yd * NZ, NZ), other], R.at[pl.ds(yd * NZ, NZ)], ps.at[i], sib)

    def pgot(i):
        yd = (y + NY + GROUPS[i]) % NY
        got(R.at[pl.ds(yd * NZ, NZ)], ps.at[i], sib)

    def sum_step(d, s, p):
        yd = (y + 4 - s) % NY if d == 0 else (y + NY - 4 + s) % NY
        q = pl.ds(yd * NZ + pb[p], 2)
        val = PS[q, core] + R[q]
        if not (s == 0 or (s == 1 and p != d)):
            got(RB.at[d, s - 1, p], ry.at[d, s - 1, p], ydev[1 - d])
            val = val + RB[d, s - 1, p].astype(F32)
        SB[d, s, p] = val.astype(BF16)
        put(SB.at[d, s, p], RB.at[d, s, p], ry.at[d, s, p], ydev[d])

    S[0] = jnp.zeros((TILE, D), F32)

    def running(lo, hi):
        def one(k, acc):
            keep = jnp.where(order[1, k] == order[1, jnp.maximum(k - 1, 0)], 1.0, 0.0)
            acc = acc * keep + Q[order[0, k]]
            S[k + 1] = acc
            return acc

        lax.fori_loop(lo, hi, one, jnp.zeros((TILE, D), F32), unroll=2)

    def user_sum(h_, x_):
        r = h_ * NX + x_
        return S[order[2, r]] + S[order[3, r]]

    zgot(1)
    xfirst(0)
    zgot(3)
    zgot(2)
    xfirst(1)
    r = X.at[pl.ds(y * NZ, NZ), core]
    put(r, r, xs.at[0, 4, 0], sib)

    fetch[5].wait()
    flips(0, 16)
    items_pass(0, 0)
    items_pass(0, 1)
    for j in (1, 2):
        got(U.at[hrel[j] * NX + x], uz.at[j - 1], hdev[j])
        users_x(j)
    flips(16, 32)
    r = X.at[pl.ds(y * NZ, NZ), other]
    got(r, xs.at[0, 4, 0], sib)
    products(y)
    items_pass(1, 0)
    items_pass(1, 1)
    items_sib(0)
    products((y + 1) % NY)
    products((y + NY - 1) % NY)
    for j in (0, 1, 2):
        for e in (1, 2, 3):
            got(U.at[hrel[j] * NX + xrel[e]], ux.at[3 - e, j], xdev[e])
    for i in (0, 1, 2):
        partial(i)
    items_pass(2, 0)
    items_pass(2, 1)
    for i in range(3, 8):
        partial(i)

    pgot(0)
    sum_step(0, 0, 0)
    sum_step(1, 0, 1)
    pgot(1)
    pgot(2)
    sum_step(0, 1, 1)
    sum_step(1, 1, 0)

    items_sib(1)
    products((y + 2) % NY)
    products((y + NY - 2) % NY)
    items_pass(3, 0)
    items_pass(3, 1)
    items_sib(2)
    products((y + 3) % NY)
    products((y + NY - 3) % NY)
    sum_step(0, 1, 0)
    sum_step(1, 1, 1)
    ocopy.wait()
    running(0, NT - 2 * NZ)
    items_sib(3)
    products((y + 4) % NY)
    running(NT - 2 * NZ, NT)

    for j in (1, 2, 0):
        for e in (2, 1, 3):
            VS[e - 1, j] = user_sum(hrel[j], xrel[e]).astype(BF16)
            put(VS.at[e - 1, j], VR.at[e - 1, j], v0.at[e - 1, j], xdev[e])

    pgot(3)
    pgot(4)
    for p in (0, 1):
        for d in (0, 1):
            sum_step(d, 2, p)

    def user_total(j):
        t = user_sum(hrel[j], x)
        for e in (1, 2, 3):
            got(VR.at[e - 1, j], v0.at[e - 1, j], xdev[NX - e])
            t = t + VR[e - 1, j].astype(F32)
        return t

    for j in (1, 2):
        US[j - 1] = user_total(j).astype(BF16)
        put(US.at[j - 1], UR.at[2 - j], vz.at[2 - j], hdev[j])

    pgot(5)
    pgot(6)
    for p in (0, 1):
        for d in (0, 1):
            sum_step(d, 3, p)

    utot = user_total(0)

    pgot(7)
    for p in (0, 1):
        for d in (0, 1):
            got(RB.at[d, 3, p], ry.at[d, 3, p], ydev[1 - d])
        q = pl.ds(y * NZ + pb[p], 2)
        ZS[pl.ds(pb[p], 2)] = (
            PS[q, core] + R[q] + RB[0, 3, p].astype(F32) + RB[1, 3, p].astype(F32)
        )
        if p == 0:
            put(ZS.at[zrel[1]], ZR.at[0], rz.at[0], zdev[1])
    for k in (2, 3):
        put(ZS.at[zrel[k]], ZR.at[k - 1], rz.at[k - 1], zdev[k])

    for j in (1, 2):
        got(UR.at[j - 1], vz.at[j - 1], hdev[j])
        utot = utot + UR[j - 1].astype(F32)
    uo[...] = 0.5 * (ue[...] + uscale * utot)

    acc = ZS[zl]
    for k in (1, 2, 3):
        got(ZR.at[k - 1], rz.at[k - 1], zdev[k])
        acc = acc + ZR[k - 1]
    io[...] = 0.5 * (ie[...] + iscale * acc)

    for c in sends:
        c.wait_send()


def on_device(user_embed, item_embed, user_degree, item_degree, tile_values, tile_rows):
    vm = pl.BlockSpec(memory_space=pltpu.VMEM)
    dma = pltpu.SemaphoreType.DMA
    user_out, item_out = pl.pallas_call(
        kernel,
        out_shape=(
            jax.ShapeDtypeStruct((TILE, D), F32),
            jax.ShapeDtypeStruct((HALF, D), F32),
        ),
        in_specs=[pl.BlockSpec(memory_space=pltpu.HBM)] * 6,
        out_specs=(vm, vm),
        scratch_shapes=[
            pltpu.VMEM((COLS, NC, HALF, D), BF16),
            pltpu.VMEM((ROWS + 1, TILE, D), BF16),
            pltpu.VMEM((NT, TILE, TILE), BF16),
            pltpu.VMEM((COLS, TILE, SLOTS * TILE), BF16),
            pltpu.VMEM((NT, TILE, D), F32),
            pltpu.VMEM((NT + 1, TILE, D), F32),
            pltpu.VMEM((COLS, NC, HALF, D), F32),
            pltpu.VMEM((COLS, HALF, D), F32),
            pltpu.VMEM((2, 4, 2, 2, HALF, D), BF16),
            pltpu.VMEM((2, 4, 2, 2, HALF, D), BF16),
            pltpu.VMEM((NZ, HALF, D), F32),
            pltpu.VMEM((NZ - 1, HALF, D), F32),
            pltpu.VMEM((NX - 1, NH, TILE, D), BF16),
            pltpu.VMEM((NX - 1, NH, TILE, D), BF16),
            pltpu.VMEM((2, TILE, D), BF16),
            pltpu.VMEM((2, TILE, D), BF16),
            pltpu.VMEM((NT, 128), jnp.int32),
            pltpu.VMEM((8, 128), jnp.int32),
            pltpu.VMEM((TILE, D), F32),
            pltpu.VMEM((HALF, D), F32),
            pltpu.VMEM((1, TILE), jnp.int32),
            pltpu.VMEM((1, HALF), jnp.int32),
            pltpu.SMEM((8, 128), jnp.int32),
            pltpu.SMEM((SLOTS, COLS), jnp.int32),
            dma((6,)),
            dma(()),
            dma((96,)),
            dma((3,)),
            dma((2, 4, 2)),
            dma((2, 5, 2)),
            dma((2,)),
            dma((3, 3)),
            dma((8,)),
            dma((2, 4, 2)),
            dma((3,)),
            dma((3, 3)),
            dma((2,)),
        ],
        compiler_params=pltpu.CompilerParams(
            collective_id=0, has_side_effects=True, vmem_limit_bytes=62 << 20
        ),
    )(
        user_embed,
        item_embed[0],
        user_degree.reshape(1, TILE),
        item_degree,
        tile_values.reshape(NT, TILE, TILE),
        tile_rows.T,
    )
    return user_out, item_out[None]


def solution(mesh):
    return jax.shard_map(
        on_device,
        mesh=mesh,
        in_specs=(
            P(("blk", "grp"), None),
            P("grp", "blk", None),
            P(("blk", "grp")),
            P("grp", "blk"),
            P("blk", "grp", None, None),
            P("blk", "grp"),
        ),
        out_specs=(P(("blk", "grp"), None), P("grp", "blk", None)),
        check_vma=False,
    )
```

```python
import jax
import jax.numpy as jnp
from jax import lax
from jax.experimental import pallas as pl
from jax.experimental.pallas import tpu as pltpu
from jax.sharding import PartitionSpec as P

NZ, NY, NC = 4, 8, 2
NH, NX = 3, 4
TILE = 128
HALF = 64
D = 256
COLS = NZ * NY
SLOTS = 2
NT = COLS * SLOTS
ROWS = NH * NX
F32, BF16 = jnp.float32, jnp.bfloat16
MESH = pl.DeviceIdType.MESH
GROUPS = (4, 3, -3, 2, -2, 1, -1, 0)

ORDER = (
    ("flip", 0), ("flip", 1), ("flip", 2), ("flip", 3), ("sort",), ("zf", 0), ("zf", 1),
    ("prod", 0), ("ip", 0, 0, 0), ("ip", 1, 0, 0), ("uz", 1, 0), ("uz", 2, 0), ("ip", 0, 0, 1),
    ("ip", 1, 0, 1), ("prod", -1), ("prod", 1), ("uz", 1, 1), ("uz", 2, 1), ("ip", 0, 1, 0),
    ("ip", 1, 1, 0), ("ip", 0, 1, 1), ("ip", 1, 1, 1), ("prod", -2), ("prod", 2), ("ip", 0, 2, 0),
    ("ip", 1, 2, 0), ("part", 0), ("part", 1), ("part", 2), ("part", 3), ("part", 4),
    ("ip", 0, 2, 1), ("ip", 1, 2, 1), ("part", 5), ("r4", 0), ("r4", 1), ("r3", 0, 0),
    ("r3", 0, 1), ("part", 6), ("r3", 1, 1), ("r3", 1, 0), ("part", 7), ("prod", -3),
    ("ip", 0, 3, 0), ("prod", 3), ("run", 0), ("r1", 0, 0), ("r1", 0, 1), ("r1", 1, 0),
    ("ip", 1, 3, 1), ("r1", 1, 1), ("prod", 4), ("run", 1), ("vs", 1, 0), ("vs", 1, 1),
    ("vs", 2, 0), ("r2", 0, 0), ("vs", 2, 1), ("vs", 0, 0), ("r2", 1, 1), ("vs", 0, 1),
    ("r2", 0, 1), ("r2", 1, 0), ("vz", 1, 0), ("vz", 1, 1), ("vz", 2, 0), ("vz", 2, 1), ("fin", 0),
    ("fin", 1), ("iout",), ("uout",),
)


def valid_gather(d, s, p):
    return s <= 2 or (s == 3 and p == d)


def column(row):
    n = row.shape[1]
    a = lax.broadcasted_iota(jnp.int32, (n, n), 0)
    b = lax.broadcasted_iota(jnp.int32, (n, n), 1)
    return jnp.sum(jnp.where(a == b, jnp.broadcast_to(row, (n, n)), 0.0), axis=1, keepdims=True)


def kernel(
    ue_h, ie_h, ud_h, ideg_h, tv, rows_h, uo, io,
    X, U, T, TT, Q, S, PS, R, SB, RB, ZS, ZB, ZR, VS, VR, US, UR, keys, plan, ue, ie, ud, ideg, uov, iov, order, rows,
    isem, osem, wsem, send, xz, xy, xs, uz, ux, ps, ry, rz, v0, vz,
):
    b = lax.axis_index("blk")
    g = lax.axis_index("grp")
    core = b % 2
    y = (b // 2) % NY
    zl = b // (2 * NY)
    x = g % NX
    zh = g // NX
    other = 1 - core

    def blk(z_, y_, c_):
        return {"blk": (z_ * NY + y_) * NC + c_}

    def grp(h_, x_):
        return {"grp": h_ * NX + x_}

    sib = blk(zl, y, other)
    ydev = (blk(zl, (y + 1) % NY, core), blk(zl, (y + NY - 1) % NY, core))
    y2dev = (blk(zl, (y + 2) % NY, core), blk(zl, (y + NY - 2) % NY, core))
    zrel = (zl, zl + 1 - 2 * (zl % 2), (zl + 2) % NZ, NZ - 1 - zl)
    zdev = tuple(blk(z_, y, core) for z_ in zrel)
    xrel = tuple((x + e) % NX for e in range(NX))
    xdev = tuple(grp(zh, x_) for x_ in xrel)
    hrel = (zh, (zh + NH - 1) % NH, (zh + 1) % NH)
    hdev = (None, grp(hrel[1], x), grp(hrel[2], x))
    pb0 = (zl // 2) * 2
    pb = (pb0, 2 - pb0)

    bar = pltpu.get_barrier_semaphore()
    peers = (sib,) + ydev + y2dev + zdev[1:] + xdev[1:] + hdev[1:]
    for dev in peers:
        pl.semaphore_signal(bar, inc=1, device_id=dev, device_id_type=MESH)

    fetch = [
        pltpu.make_async_copy(a, v, isem.at[n])
        for n, (a, v) in enumerate(
            ((ideg_h, ideg), (ud_h, ud), (ie_h, ie), (ue_h, ue), (rows_h, rows), (tv, T))
        )
    ]
    for c in fetch:
        c.start()

    sends = []

    def put(src, dst, rsem, dev):
        c = pltpu.make_async_remote_copy(
            src_ref=src, dst_ref=dst, send_sem=send.at[len(sends)], recv_sem=rsem,
            device_id=dev, device_id_type=MESH,
        )
        c.start()
        sends.append(c)

    def got(dst, rsem, dev):
        pltpu.make_async_remote_copy(
            src_ref=dst, dst_ref=dst, send_sem=send.at[0], recv_sem=rsem,
            device_id=dev, device_id_type=MESH,
        ).wait_recv()

    for c in fetch[:4]:
        c.wait()
    iscale = column(lax.rsqrt(ideg[...].astype(F32)))
    uscale = column(lax.rsqrt(ud[...].astype(F32)))
    X[y * NZ + zl, core] = (ie[...] * iscale).astype(BF16)
    U[g] = (ue[...] * uscale).astype(BF16)
    U[ROWS] = jnp.zeros((TILE, D), BF16)

    pl.semaphore_wait(bar, len(peers))

    own = X.at[y * NZ + zl, core]
    for k in (1, 3, 2):
        put(own, own, xz.at[k - 1], zdev[k])
    def urows(j, x_, q):
        return U.at[hrel[j] * NX + x_, pl.ds(q * HALF, HALF)]

    for q in (0, 1):
        for j in (1, 2):
            put(urows(0, x, q), urows(0, x, q), uz.at[2 - j, q], hdev[j])
    for e in (2, 1, 3):
        put(U.at[g], U.at[g], ux.at[e - 1, 0, 0], xdev[e])

    def xreg(yy, p, c):
        return X.at[pl.ds(yy * NZ + pb[p], 2), c]

    def yfrom(d, s):
        return (y + NY - 1 - s) % NY if d == 0 else (y + 1 + s) % NY

    ocopy = pltpu.make_async_copy(plan, order, osem)

    def total(m, v):
        return jnp.sum(jnp.where(m, v, 0), axis=0, keepdims=True)

    def do_sort():
        fetch[4].wait()
        for i in range(NT):
            keys[i : i + 1, :] = jnp.full((1, 128), rows[i % SLOTS, i // SLOTS], jnp.int32)
        sub = lax.broadcasted_iota(jnp.int32, (NT, 128), 0)
        lane = lax.broadcasted_iota(jnp.int32, (NT, 128), 1)
        late = (sub // SLOTS) % NY == (y + 4) % NY
        kc = keys[...]
        kl = jnp.where(late, kc + 16, kc)
        uc = kl * NT + sub
        ur = jnp.sum(jnp.where(sub == lane, uc, 0), axis=0, keepdims=True)
        ur = jnp.where(lax.broadcasted_iota(jnp.int32, (1, 128), 1) < NT, ur, 1 << 20)
        rank = jnp.sum(jnp.where(ur < uc, 1, 0), axis=1, keepdims=True)
        hit = rank == lane

        plan[...] = jnp.zeros((8, 128), jnp.int32)
        plan[0:1, :] = total(hit, sub)
        plan[1:2, :] = total(hit, kl)
        plan[2:3, :] = jnp.where(total(kl == lane, 1) > 0, total(kl <= lane, 1), 0)
        plan[3:4, :] = jnp.where(total(kl == lane + 16, 1) > 0, total(kl <= lane + 16, 1), 0)
        ocopy.start()

    def xfirst(p):
        for d in (0, 1):
            put(xreg(y, p, core), xreg(y, p, core), xy.at[d, 0, p], ydev[d])

    def zgot(k):
        r = X.at[y * NZ + zrel[k], core]
        got(r, xz.at[k - 1], zdev[k])

    def flip(c, _):
        TT[c, :, 0:TILE] = T[2 * c].T
        TT[c, :, TILE:] = T[2 * c + 1].T
        return 0

    def flips(lo, hi):
        lax.fori_loop(lo, hi, flip, 0, unroll=2)

    def products(yy):
        def one(z_, _):
            c = z_ * NY + yy
            lhs = T[pl.ds(2 * c, 2)].reshape(SLOTS * TILE, TILE)
            out = jnp.dot(lhs, X[yy * NZ + z_].reshape(TILE, D), preferred_element_type=F32)
            Q[pl.ds(2 * c, 2)] = out.reshape(SLOTS, TILE, D)
            return 0

        lax.fori_loop(0, NZ, one, 0, unroll=2)

    def do_part(i):
        yd = (y + NY + GROUPS[i]) % NY
        if i == 0:
            for e in (1, 2, 3):
                got(U.at[hrel[0] * NX + xrel[e]], ux.at[3 - e, 0, 0], xdev[e])
                for j in (1, 2):
                    for q in (0, 1):
                        got(urows(j, xrel[e], q), ux.at[3 - e, j, q], xdev[e])

        def one(z_, _):
            c = z_ * NY + yd
            rhs = jnp.concatenate([U[rows[0, c]], U[rows[1, c]]], axis=0)
            out = jnp.dot(TT[c], rhs, preferred_element_type=F32)
            PS[yd * NZ + z_] = out.reshape(NC, HALF, D)
            return 0

        lax.fori_loop(0, NZ, one, 0, unroll=2)
        put(PS.at[pl.ds(yd * NZ, NZ), other], R.at[pl.ds(yd * NZ, NZ)], ps.at[i], sib)

    have = set()

    def both(n, d, p):
        i = GROUPS.index(n if d == 0 or n == 4 else -n)
        yd = (y + NY + GROUPS[i]) % NY
        if i not in have:
            have.add(i)
            got(R.at[pl.ds(yd * NZ, NZ)], ps.at[i], sib)
        q = pl.ds(yd * NZ + pb[p], 2)
        return PS[q, core] + R[q]

    def pass_on(val, d, n, dev):
        SB[d, n] = val.astype(BF16)
        put(SB.at[d, n], RB.at[d, n], ry.at[d, n], dev)

    def came(d, n):
        got(RB.at[d, n], ry.at[d, n], ydev[1 - d])
        return RB[d, n].astype(F32)

    def do_r4(d):
        pass_on(both(4, d, d), d, 0, y2dev[d])

    def do_r3(d, p):
        pass_on(both(3, d, p), d, 1 + p, ydev[d])

    def do_r2(d, p):
        val = both(2, d, p) + came(d, 1 + p)
        if p == d:
            val = val + came(d, 0)
        pass_on(val, d, 3 + p, y2dev[d])

    def do_r1(d, p):
        pass_on(both(1, d, p), d, 5 + p, ydev[d])

    def do_fin(p):
        val = both(0, 0, p)
        for d in (0, 1):
            val = val + came(d, 3 + p) + came(d, 5 + p)
        ZS[pl.ds(pb[p], 2)] = val
        ZB[pl.ds(pb[p], 2)] = val.astype(BF16)
        for k in ((1,), (2, 3))[p]:
            put(ZB.at[zrel[k]], ZR.at[k - 1], rz.at[k - 1], zdev[k])

    S[0] = jnp.zeros((TILE, D), F32)

    def running(lo, hi):
        def one(k, acc):
            keep = jnp.where(order[1, k] == order[1, jnp.maximum(k - 1, 0)], 1.0, 0.0)
            acc = acc * keep + Q[order[0, k]]
            S[k + 1] = acc
            return acc

        lax.fori_loop(lo, hi, one, jnp.zeros((TILE, D), F32), unroll=2)

    def do_run(late):
        if late:
            running(NT - 2 * NZ, NT)
        else:
            ocopy.wait()
            running(0, NT - 2 * NZ)

    def user_sum(j, x_, q):
        r = hrel[j] * NX + x_
        w = pl.ds(q * HALF, HALF)
        return S[order[2, r], w] + S[order[3, r], w]

    def do_zf(p):
        for k in ((1,), (3, 2))[p]:
            zgot(k)
        xfirst(p)
        if p == 1:
            r = X.at[pl.ds(y * NZ, NZ), core]
            put(r, r, xs.at[0, 4, 0], sib)

    def do_flip(i):
        if i == 0:
            fetch[5].wait()
        flips(i * COLS // 4, (i + 1) * COLS // 4)

    def do_ip(d, s, p):
        r = xreg(yfrom(d, s), p, core)
        got(r, xy.at[d, s, p], ydev[1 - d])
        if valid_gather(d, s + 1, p):
            put(r, r, xy.at[d, s + 1, p], ydev[d])
        put(r, r, xs.at[d, s, p], sib)

    def do_uz(j, q):
        r = urows(j, x, q)
        got(r, uz.at[j - 1, q], hdev[j])
        for e in (2, 1, 3):
            put(r, r, ux.at[e - 1, j, q], xdev[e])

    def do_prod(off):
        if off == 0:
            r = X.at[pl.ds(y * NZ, NZ), other]
            got(r, xs.at[0, 4, 0], sib)
        else:
            s = abs(off) - 1
            for d in (0, 1):
                for p in (0, 1):
                    if off == 4 and p == d or off != 4 and d == (off > 0):
                        got(xreg(yfrom(d, s), p, other), xs.at[d, s, p], sib)
        products((y + NY + off) % NY)

    def do_vs(j, q):
        w = pl.ds(q * HALF, HALF)
        for e in (2, 1, 3):
            VS[e - 1, j, w] = user_sum(j, xrel[e], q).astype(BF16)
            put(VS.at[e - 1, j, w], VR.at[e - 1, j, w], v0.at[e - 1, j, q], xdev[e])

    def user_total(j, q):
        w = pl.ds(q * HALF, HALF)
        t = user_sum(j, x, q)
        for e in (1, 2, 3):
            got(VR.at[e - 1, j, w], v0.at[e - 1, j, q], xdev[NX - e])
            t = t + VR[e - 1, j, w].astype(F32)
        return t

    def do_vz(j, q):
        w = pl.ds(q * HALF, HALF)
        US[j - 1, w] = user_total(j, q).astype(BF16)
        put(US.at[j - 1, w], UR.at[2 - j, w], vz.at[2 - j, q], hdev[j])

    out = [pltpu.make_async_copy(uov, uo, wsem.at[0]), pltpu.make_async_copy(iov, io, wsem.at[1])]

    def do_uout():
        for q in (0, 1):
            w = slice(q * HALF, (q + 1) * HALF)
            t = user_total(0, q)
            for j in (1, 2):
                got(UR.at[j - 1, pl.ds(q * HALF, HALF)], vz.at[j - 1, q], hdev[j])
                t = t + UR[j - 1, w].astype(F32)
            uov[w] = 0.5 * (ue[w] + uscale[w] * t)
        out[0].start()

    def do_iout():
        acc = ZS[zl]
        for k in (1, 2, 3):
            got(ZR.at[k - 1], rz.at[k - 1], zdev[k])
            acc = acc + ZR[k - 1].astype(F32)
        iov[...] = 0.5 * (ie[...] + iscale * acc)
        out[1].start()

    steps = {
        "zf": do_zf, "sort": do_sort, "flip": do_flip, "ip": do_ip, "uz": do_uz, "part": do_part,
        "prod": do_prod, "run": do_run, "r4": do_r4, "r3": do_r3, "r2": do_r2, "r1": do_r1,
        "fin": do_fin, "vs": do_vs, "vz": do_vz, "uout": do_uout, "iout": do_iout,
    }
    for name, *at in ORDER:
        steps[name](*at)

    for c in out:
        c.wait()
    for c in sends:
        c.wait_send()


def hand_over(a, b, c, d, sem):
    copies = [pltpu.make_async_copy(a, c, sem.at[0]), pltpu.make_async_copy(b, d, sem.at[1])]
    for c in copies:
        c.start()
    for c in copies:
        c.wait()


def on_device(user_embed, item_embed, user_degree, item_degree, tile_values, tile_rows):
    hbm = pl.BlockSpec(memory_space=pltpu.HBM)
    dma = pltpu.SemaphoreType.DMA
    shapes = (
        jax.ShapeDtypeStruct((TILE, D), F32),
        jax.ShapeDtypeStruct((HALF, D), F32),
    )
    user_out, item_out = pl.pallas_call(
        kernel,
        out_shape=shapes,
        in_specs=[hbm] * 6,
        out_specs=(hbm, hbm),
        scratch_shapes=[
            pltpu.VMEM((COLS, NC, HALF, D), BF16),
            pltpu.VMEM((ROWS + 1, TILE, D), BF16),
            pltpu.VMEM((NT, TILE, TILE), BF16),
            pltpu.VMEM((COLS, TILE, SLOTS * TILE), BF16),
            pltpu.VMEM((NT, TILE, D), F32),
            pltpu.VMEM((NT + 1, TILE, D), F32),
            pltpu.VMEM((COLS, NC, HALF, D), F32),
            pltpu.VMEM((COLS, HALF, D), F32),
            pltpu.VMEM((2, 7, 2, HALF, D), BF16),
            pltpu.VMEM((2, 7, 2, HALF, D), BF16),
            pltpu.VMEM((NZ, HALF, D), F32),
            pltpu.VMEM((NZ, HALF, D), BF16),
            pltpu.VMEM((NZ - 1, HALF, D), BF16),
            pltpu.VMEM((NX - 1, NH, TILE, D), BF16),
            pltpu.VMEM((NX - 1, NH, TILE, D), BF16),
            pltpu.VMEM((2, TILE, D), BF16),
            pltpu.VMEM((2, TILE, D), BF16),
            pltpu.VMEM((NT, 128), jnp.int32),
            pltpu.VMEM((8, 128), jnp.int32),
            pltpu.VMEM((TILE, D), F32),
            pltpu.VMEM((HALF, D), F32),
            pltpu.VMEM((1, TILE), jnp.int32),
            pltpu.VMEM((1, HALF), jnp.int32),
            pltpu.VMEM((TILE, D), F32),
            pltpu.VMEM((HALF, D), F32),
            pltpu.SMEM((8, 128), jnp.int32),
            pltpu.SMEM((SLOTS, COLS), jnp.int32),
            dma((6,)),
            dma(()),
            dma((2,)),
            dma((104,)),
            dma((3,)),
            dma((2, 4, 2)),
            dma((2, 5, 2)),
            dma((2, 2)),
            dma((3, 3, 2)),
            dma((8,)),
            dma((2, 7)),
            dma((3,)),
            dma((3, 3, 2)),
            dma((2, 2)),
        ],
        compiler_params=pltpu.CompilerParams(
            collective_id=0, has_side_effects=True, vmem_limit_bytes=62 << 20
        ),
    )(
        user_embed,
        item_embed[0],
        user_degree.reshape(1, TILE),
        item_degree,
        tile_values.reshape(NT, TILE, TILE),
        tile_rows.T,
    )
    user_out, item_out = pl.pallas_call(
        hand_over,
        out_shape=shapes,
        in_specs=[hbm] * 2,
        out_specs=(hbm, hbm),
        scratch_shapes=[dma((2,))],
        compiler_params=pltpu.CompilerParams(vmem_limit_bytes=62 << 20),
    )(user_out, item_out)
    return user_out, item_out[None]


def solution(mesh):
    return jax.shard_map(
        on_device,
        mesh=mesh,
        in_specs=(
            P(("blk", "grp"), None),
            P("grp", "blk", None),
            P(("blk", "grp")),
            P("grp", "blk"),
            P("blk", "grp", None, None),
            P("blk", "grp"),
        ),
        out_specs=(P(("blk", "grp"), None), P("grp", "blk", None)),
        check_vma=False,
    )
```

```python
import jax
import jax.numpy as jnp
from jax import lax
from jax.experimental import pallas as pl
from jax.experimental.pallas import tpu as pltpu
from jax.sharding import PartitionSpec as P

NZ, NY, NC = 4, 8, 2
NH, NX = 3, 4
TILE = 128
HALF = 64
D = 256
COLS = NZ * NY
SLOTS = 2
NT = COLS * SLOTS
ROWS = NH * NX
F32, BF16 = jnp.float32, jnp.bfloat16
MESH = pl.DeviceIdType.MESH
GROUPS = (4, 3, -3, 2, -2, 1, -1, 0)

ORDER = (
    ("flip", 0), ("flip", 1), ("flip", 2), ("flip", 3), ("sort",), ("zf", 0), ("zf", 1),
    ("prod", 0), ("ip", 0, 0, 0), ("ip", 1, 0, 0), ("uz", 1, 0), ("uz", 2, 0), ("ip", 0, 0, 1),
    ("ip", 1, 0, 1), ("prod", -1), ("prod", 1), ("uz", 1, 1), ("uz", 2, 1), ("ip", 0, 1, 0),
    ("ip", 1, 1, 0), ("ip", 0, 1, 1), ("ip", 1, 1, 1), ("prod", -2), ("prod", 2), ("ip", 0, 2, 0),
    ("ip", 1, 2, 0), ("part", 0), ("part", 1), ("part", 2), ("part", 3), ("part", 4),
    ("ip", 0, 2, 1), ("ip", 1, 2, 1), ("part", 5), ("r4", 0), ("r4", 1), ("r3", 0, 0),
    ("r3", 0, 1), ("part", 6), ("r3", 1, 1), ("r3", 1, 0), ("part", 7), ("prod", -3),
    ("ip", 0, 3, 0), ("prod", 3), ("run", 0), ("r1", 0, 0), ("r1", 0, 1), ("r1", 1, 0),
    ("ip", 1, 3, 1), ("r1", 1, 1), ("prod", 4), ("run", 1), ("vs", 1, 0), ("vs", 1, 1),
    ("vs", 2, 0), ("r2", 0, 0), ("vs", 2, 1), ("vs", 0, 0), ("r2", 1, 1), ("vs", 0, 1),
    ("r2", 0, 1), ("r2", 1, 0), ("vz", 1, 0), ("vz", 1, 1), ("vz", 2, 0), ("vz", 2, 1), ("fin", 0),
    ("fin", 1), ("iout",), ("uout",),
)
QU, QV = 2, 2


def valid_gather(d, s, p):
    return s <= 2 or (s == 3 and p == d)


def column(row):
    n = row.shape[1]
    a = lax.broadcasted_iota(jnp.int32, (n, n), 0)
    b = lax.broadcasted_iota(jnp.int32, (n, n), 1)
    return jnp.sum(jnp.where(a == b, jnp.broadcast_to(row, (n, n)), 0.0), axis=1, keepdims=True)


def kernel(
    ue_h, ie_h, ud_h, ideg_h, tv, rows_h, uo, io,
    X, U, T, TT, Q, S, PS, R, SB, RB, ZS, ZB, ZR, VS, VR, US, UR, keys, plan, ue, ie, ud, ideg, uov, iov, order, rows,
    isem, osem, wsem, send, xz, xy, xs, uz, ux, ps, ry, rz, v0, vz,
):
    b = lax.axis_index("blk")
    g = lax.axis_index("grp")
    core = b % 2
    y = (b // 2) % NY
    zl = b // (2 * NY)
    x = g % NX
    zh = g // NX
    other = 1 - core

    def blk(z_, y_, c_):
        return {"blk": (z_ * NY + y_) * NC + c_}

    def grp(h_, x_):
        return {"grp": h_ * NX + x_}

    sib = blk(zl, y, other)
    ydev = (blk(zl, (y + 1) % NY, core), blk(zl, (y + NY - 1) % NY, core))
    y2dev = (blk(zl, (y + 2) % NY, core), blk(zl, (y + NY - 2) % NY, core))
    zrel = (zl, zl + 1 - 2 * (zl % 2), (zl + 2) % NZ, NZ - 1 - zl)
    zdev = tuple(blk(z_, y, core) for z_ in zrel)
    xrel = tuple((x + e) % NX for e in range(NX))
    xdev = tuple(grp(zh, x_) for x_ in xrel)
    hrel = (zh, (zh + NH - 1) % NH, (zh + 1) % NH)
    hdev = (None, grp(hrel[1], x), grp(hrel[2], x))
    pb0 = (zl // 2) * 2
    pb = (pb0, 2 - pb0)

    PART = TILE // QV
    bar = pltpu.get_barrier_semaphore()
    peers = (sib,) + ydev + y2dev + zdev[1:] + xdev[1:] + hdev[1:]
    for dev in peers:
        pl.semaphore_signal(bar, inc=1, device_id=dev, device_id_type=MESH)

    fetch = [
        pltpu.make_async_copy(a, v, isem.at[n])
        for n, (a, v) in enumerate(
            ((ideg_h, ideg), (ud_h, ud), (ie_h, ie), (ue_h, ue), (rows_h, rows), (tv, T))
        )
    ]
    for c in fetch:
        c.start()

    sends = []

    def put(src, dst, rsem, dev):
        c = pltpu.make_async_remote_copy(
            src_ref=src, dst_ref=dst, send_sem=send.at[len(sends)], recv_sem=rsem,
            device_id=dev, device_id_type=MESH,
        )
        c.start()
        sends.append(c)

    def got(dst, rsem, dev):
        pltpu.make_async_remote_copy(
            src_ref=dst, dst_ref=dst, send_sem=send.at[0], recv_sem=rsem,
            device_id=dev, device_id_type=MESH,
        ).wait_recv()

    for c in fetch[:4]:
        c.wait()
    iscale = column(lax.rsqrt(ideg[...].astype(F32)))
    uscale = column(lax.rsqrt(ud[...].astype(F32)))
    X[y * NZ + zl, core] = (ie[...] * iscale).astype(BF16)
    U[g] = (ue[...] * uscale).astype(BF16)
    U[ROWS] = jnp.zeros((TILE, D), BF16)

    pl.semaphore_wait(bar, len(peers))

    own = X.at[y * NZ + zl, core]
    for k in (1, 3, 2):
        put(own, own, xz.at[k - 1], zdev[k])
    def urows(j, x_, q):
        return U.at[hrel[j] * NX + x_, pl.ds(q * (TILE // QU), TILE // QU)]

    for q in range(QU):
        for j in (1, 2):
            put(urows(0, x, q), urows(0, x, q), uz.at[2 - j, q], hdev[j])
    for e in (2, 1, 3):
        put(U.at[g], U.at[g], ux.at[e - 1, 0, 0], xdev[e])

    def xreg(yy, p, c):
        return X.at[pl.ds(yy * NZ + pb[p], 2), c]

    def yfrom(d, s):
        return (y + NY - 1 - s) % NY if d == 0 else (y + 1 + s) % NY

    ocopy = pltpu.make_async_copy(plan, order, osem)

    def total(m, v):
        return jnp.sum(jnp.where(m, v, 0), axis=0, keepdims=True)

    def do_sort():
        fetch[4].wait()
        for i in range(NT):
            keys[i : i + 1, :] = jnp.full((1, 128), rows[i % SLOTS, i // SLOTS], jnp.int32)
        sub = lax.broadcasted_iota(jnp.int32, (NT, 128), 0)
        lane = lax.broadcasted_iota(jnp.int32, (NT, 128), 1)
        late = (sub // SLOTS) % NY == (y + 4) % NY
        kc = keys[...]
        kl = jnp.where(late, kc + 16, kc)
        uc = kl * NT + sub
        ur = jnp.sum(jnp.where(sub == lane, uc, 0), axis=0, keepdims=True)
        ur = jnp.where(lax.broadcasted_iota(jnp.int32, (1, 128), 1) < NT, ur, 1 << 20)
        rank = jnp.sum(jnp.where(ur < uc, 1, 0), axis=1, keepdims=True)
        hit = rank == lane

        plan[...] = jnp.zeros((8, 128), jnp.int32)
        plan[0:1, :] = total(hit, sub)
        plan[1:2, :] = total(hit, kl)
        plan[2:3, :] = jnp.where(total(kl == lane, 1) > 0, total(kl <= lane, 1), 0)
        plan[3:4, :] = jnp.where(total(kl == lane + 16, 1) > 0, total(kl <= lane + 16, 1), 0)
        ocopy.start()

    def xfirst(p):
        for d in (0, 1):
            put(xreg(y, p, core), xreg(y, p, core), xy.at[d, 0, p], ydev[d])

    def zgot(k):
        r = X.at[y * NZ + zrel[k], core]
        got(r, xz.at[k - 1], zdev[k])

    def flip(c, _):
        TT[c, :, 0:TILE] = T[2 * c].T
        TT[c, :, TILE:] = T[2 * c + 1].T
        return 0

    def flips(lo, hi):
        lax.fori_loop(lo, hi, flip, 0, unroll=2)

    def products(yy):
        def one(z_, _):
            c = z_ * NY + yy
            lhs = T[pl.ds(2 * c, 2)].reshape(SLOTS * TILE, TILE)
            out = jnp.dot(lhs, X[yy * NZ + z_].reshape(TILE, D), preferred_element_type=F32)
            Q[pl.ds(2 * c, 2)] = out.reshape(SLOTS, TILE, D)
            return 0

        lax.fori_loop(0, NZ, one, 0, unroll=2)

    def do_part(i):
        yd = (y + NY + GROUPS[i]) % NY
        if i == 0:
            for e in (1, 2, 3):
                got(U.at[hrel[0] * NX + xrel[e]], ux.at[3 - e, 0, 0], xdev[e])
                for j in (1, 2):
                    for q in range(QU):
                        got(urows(j, xrel[e], q), ux.at[3 - e, j, q], xdev[e])

        def one(z_, _):
            c = z_ * NY + yd
            rhs = jnp.concatenate([U[rows[0, c]], U[rows[1, c]]], axis=0)
            out = jnp.dot(TT[c], rhs, preferred_element_type=F32)
            PS[yd * NZ + z_] = out.reshape(NC, HALF, D)
            return 0

        lax.fori_loop(0, NZ, one, 0, unroll=2)
        put(PS.at[pl.ds(yd * NZ, NZ), other], R.at[pl.ds(yd * NZ, NZ)], ps.at[i], sib)

    have = set()

    def both(n, d, p):
        i = GROUPS.index(n if d == 0 or n == 4 else -n)
        yd = (y + NY + GROUPS[i]) % NY
        if i not in have:
            have.add(i)
            got(R.at[pl.ds(yd * NZ, NZ)], ps.at[i], sib)
        q = pl.ds(yd * NZ + pb[p], 2)
        return PS[q, core] + R[q]

    def pass_on(val, d, n, dev):
        SB[d, n] = val.astype(BF16)
        put(SB.at[d, n], RB.at[d, n], ry.at[d, n], dev)

    def came(d, n):
        got(RB.at[d, n], ry.at[d, n], ydev[1 - d])
        return RB[d, n].astype(F32)

    def do_r4(d):
        pass_on(both(4, d, d), d, 0, y2dev[d])

    def do_r3(d, p):
        pass_on(both(3, d, p), d, 1 + p, ydev[d])

    def do_r2(d, p):
        val = both(2, d, p) + came(d, 1 + p)
        if p == d:
            val = val + came(d, 0)
        pass_on(val, d, 3 + p, y2dev[d])

    def do_r1(d, p):
        pass_on(both(1, d, p), d, 5 + p, ydev[d])

    def do_fin(p):
        val = both(0, 0, p)
        for d in (0, 1):
            val = val + came(d, 3 + p) + came(d, 5 + p)
        ZS[pl.ds(pb[p], 2)] = val
        ZB[pl.ds(pb[p], 2)] = val.astype(BF16)
        for k in ((1,), (2, 3))[p]:
            put(ZB.at[zrel[k]], ZR.at[k - 1], rz.at[k - 1], zdev[k])

    S[0] = jnp.zeros((TILE, D), F32)

    def running(lo, hi):
        def one(k, acc):
            keep = jnp.where(order[1, k] == order[1, jnp.maximum(k - 1, 0)], 1.0, 0.0)
            acc = acc * keep + Q[order[0, k]]
            S[k + 1] = acc
            return acc

        lax.fori_loop(lo, hi, one, jnp.zeros((TILE, D), F32), unroll=2)

    def do_run(late):
        if late:
            running(NT - 2 * NZ, NT)
        else:
            ocopy.wait()
            running(0, NT - 2 * NZ)

    def user_sum(j, x_, q):
        r = hrel[j] * NX + x_
        w = pl.ds(q * PART, PART)
        return S[order[2, r], w] + S[order[3, r], w]

    def do_zf(p):
        for k in ((1,), (3, 2))[p]:
            zgot(k)
        xfirst(p)
        if p == 1:
            r = X.at[pl.ds(y * NZ, NZ), core]
            put(r, r, xs.at[0, 4, 0], sib)

    def do_flip(i):
        if i == 0:
            fetch[5].wait()
        flips(i * COLS // 4, (i + 1) * COLS // 4)

    def do_ip(d, s, p):
        r = xreg(yfrom(d, s), p, core)
        got(r, xy.at[d, s, p], ydev[1 - d])
        if valid_gather(d, s + 1, p):
            put(r, r, xy.at[d, s + 1, p], ydev[d])
        put(r, r, xs.at[d, s, p], sib)

    def do_uz(j, q):
        r = urows(j, x, q)
        got(r, uz.at[j - 1, q], hdev[j])
        for e in (2, 1, 3):
            put(r, r, ux.at[e - 1, j, q], xdev[e])

    def do_prod(off):
        if off == 0:
            r = X.at[pl.ds(y * NZ, NZ), other]
            got(r, xs.at[0, 4, 0], sib)
        else:
            s = abs(off) - 1
            for d in (0, 1):
                for p in (0, 1):
                    if off == 4 and p == d or off != 4 and d == (off > 0):
                        got(xreg(yfrom(d, s), p, other), xs.at[d, s, p], sib)
        products((y + NY + off) % NY)

    def do_vs(j, q):
        w = pl.ds(q * PART, PART)
        for e in (2, 1, 3):
            VS[e - 1, j, w] = user_sum(j, xrel[e], q).astype(BF16)
            put(VS.at[e - 1, j, w], VR.at[e - 1, j, w], v0.at[e - 1, j, q], xdev[e])

    def user_total(j, q):
        w = pl.ds(q * PART, PART)
        t = user_sum(j, x, q)
        for e in (1, 2, 3):
            got(VR.at[e - 1, j, w], v0.at[e - 1, j, q], xdev[NX - e])
            t = t + VR[e - 1, j, w].astype(F32)
        return t

    def do_vz(j, q):
        w = pl.ds(q * PART, PART)
        US[j - 1, w] = user_total(j, q).astype(BF16)
        put(US.at[j - 1, w], UR.at[2 - j, w], vz.at[2 - j, q], hdev[j])

    out = [pltpu.make_async_copy(uov, uo, wsem.at[0]), pltpu.make_async_copy(iov, io, wsem.at[1])]

    def do_uout():
        for q in range(QV):
            w = slice(q * PART, (q + 1) * PART)
            t = user_total(0, q)
            for j in (1, 2):
                got(UR.at[j - 1, pl.ds(q * PART, PART)], vz.at[j - 1, q], hdev[j])
                t = t + UR[j - 1, w].astype(F32)
            uov[w] = 0.5 * (ue[w] + uscale[w] * t)
        out[0].start()

    def do_iout():
        acc = ZS[zl]
        for k in (1, 2, 3):
            got(ZR.at[k - 1], rz.at[k - 1], zdev[k])
            acc = acc + ZR[k - 1].astype(F32)
        iov[...] = 0.5 * (ie[...] + iscale * acc)
        out[1].start()

    steps = {
        "zf": do_zf, "sort": do_sort, "flip": do_flip, "ip": do_ip, "uz": do_uz, "part": do_part,
        "prod": do_prod, "run": do_run, "r4": do_r4, "r3": do_r3, "r2": do_r2, "r1": do_r1,
        "fin": do_fin, "vs": do_vs, "vz": do_vz, "uout": do_uout, "iout": do_iout,
    }
    for name, *at in ORDER:
        steps[name](*at)

    for c in out:
        c.wait()
    for c in sends:
        c.wait_send()


def hand_over(a, b, c, d, va, vb, sem):
    in_a = pltpu.make_async_copy(a, va, sem.at[0])
    in_b = pltpu.make_async_copy(b, vb, sem.at[1])
    out_a = pltpu.make_async_copy(va, c, sem.at[2])
    out_b = pltpu.make_async_copy(vb, d, sem.at[3])
    in_a.start()
    in_b.start()
    in_a.wait()
    out_a.start()
    in_b.wait()
    out_b.start()
    out_a.wait()
    out_b.wait()


def on_device(user_embed, item_embed, user_degree, item_degree, tile_values, tile_rows):
    hbm = pl.BlockSpec(memory_space=pltpu.HBM)
    dma = pltpu.SemaphoreType.DMA
    shapes = (
        jax.ShapeDtypeStruct((TILE, D), F32),
        jax.ShapeDtypeStruct((HALF, D), F32),
    )
    user_out, item_out = pl.pallas_call(
        kernel,
        out_shape=shapes,
        in_specs=[hbm] * 6,
        out_specs=(hbm, hbm),
        scratch_shapes=[
            pltpu.VMEM((COLS, NC, HALF, D), BF16),
            pltpu.VMEM((ROWS + 1, TILE, D), BF16),
            pltpu.VMEM((NT, TILE, TILE), BF16),
            pltpu.VMEM((COLS, TILE, SLOTS * TILE), BF16),
            pltpu.VMEM((NT, TILE, D), F32),
            pltpu.VMEM((NT + 1, TILE, D), F32),
            pltpu.VMEM((COLS, NC, HALF, D), F32),
            pltpu.VMEM((COLS, HALF, D), F32),
            pltpu.VMEM((2, 7, 2, HALF, D), BF16),
            pltpu.VMEM((2, 7, 2, HALF, D), BF16),
            pltpu.VMEM((NZ, HALF, D), F32),
            pltpu.VMEM((NZ, HALF, D), BF16),
            pltpu.VMEM((NZ - 1, HALF, D), BF16),
            pltpu.VMEM((NX - 1, NH, TILE, D), BF16),
            pltpu.VMEM((NX - 1, NH, TILE, D), BF16),
            pltpu.VMEM((2, TILE, D), BF16),
            pltpu.VMEM((2, TILE, D), BF16),
            pltpu.VMEM((NT, 128), jnp.int32),
            pltpu.VMEM((8, 128), jnp.int32),
            pltpu.VMEM((TILE, D), F32),
            pltpu.VMEM((HALF, D), F32),
            pltpu.VMEM((1, TILE), jnp.int32),
            pltpu.VMEM((1, HALF), jnp.int32),
            pltpu.VMEM((TILE, D), F32),
            pltpu.VMEM((HALF, D), F32),
            pltpu.SMEM((8, 128), jnp.int32),
            pltpu.SMEM((SLOTS, COLS), jnp.int32),
            dma((6,)),
            dma(()),
            dma((2,)),
            dma((104,)),
            dma((3,)),
            dma((2, 4, 2)),
            dma((2, 5, 2)),
            dma((2, 2)),
            dma((3, 3, 2)),
            dma((8,)),
            dma((2, 7)),
            dma((3,)),
            dma((3, 3, 2)),
            dma((2, 2)),
        ],
        compiler_params=pltpu.CompilerParams(
            collective_id=0, has_side_effects=True, vmem_limit_bytes=62 << 20
        ),
    )(
        user_embed,
        item_embed[0],
        user_degree.reshape(1, TILE),
        item_degree,
        tile_values.reshape(NT, TILE, TILE),
        tile_rows.T,
    )
    user_out, item_out = pl.pallas_call(
        hand_over,
        out_shape=shapes,
        in_specs=[hbm] * 2,
        out_specs=(hbm, hbm),
        scratch_shapes=[pltpu.VMEM((TILE, D), F32), pltpu.VMEM((HALF, D), F32), dma((4,))],
        compiler_params=pltpu.CompilerParams(vmem_limit_bytes=62 << 20),
    )(user_out, item_out)
    return user_out, item_out[None]


def solution(mesh):
    return jax.shard_map(
        on_device,
        mesh=mesh,
        in_specs=(
            P(("blk", "grp"), None),
            P("grp", "blk", None),
            P(("blk", "grp")),
            P("grp", "blk"),
            P("blk", "grp", None, None),
            P("blk", "grp"),
        ),
        out_specs=(P(("blk", "grp"), None), P("grp", "blk", None)),
        check_vma=False,
    )
```

```python
import jax
import jax.numpy as jnp
from jax import lax
from jax.experimental import pallas as pl
from jax.experimental.pallas import tpu as pltpu
from jax.sharding import PartitionSpec as P

NZ, NY, NC = 4, 8, 2
NH, NX = 3, 4
TILE = 128
HALF = 64
D = 256
COLS = NZ * NY
SLOTS = 2
NT = COLS * SLOTS
ROWS = NH * NX
F32, BF16 = jnp.float32, jnp.bfloat16
MESH = pl.DeviceIdType.MESH
GROUPS = (4, 3, -3, 2, -2, 1, -1, 0)

ORDER = (
    ("flip", 0), ("flip", 1), ("flip", 2), ("flip", 3), ("sort",), ("zf", 0), ("zf", 1),
    ("prod", 0), ("ip", 0, 0, 0), ("ip", 1, 0, 0), ("uz", 1, 0), ("uz", 2, 0), ("ip", 0, 0, 1),
    ("ip", 1, 0, 1), ("prod", -1), ("prod", 1), ("uz", 1, 1), ("uz", 2, 1), ("ip", 0, 1, 0),
    ("ip", 1, 1, 0), ("ip", 0, 1, 1), ("ip", 1, 1, 1), ("prod", -2), ("prod", 2), ("ip", 0, 2, 0),
    ("ip", 1, 2, 0), ("ip", 0, 2, 1), ("ip", 1, 2, 1), ("part", 0), ("part", 1), ("part", 2),
    ("part", 3), ("part", 4), ("part", 5), ("r4", 0), ("r4", 1), ("r3", 0, 0), ("r3", 0, 1),
    ("part", 6), ("r3", 1, 1), ("r3", 1, 0), ("part", 7), ("prod", -3), ("prod", 3),
    ("ip", 0, 3, 0), ("ip", 1, 3, 1), ("run", 0), ("r1", 0, 0), ("r1", 0, 1), ("r1", 1, 0),
    ("r1", 1, 1), ("prod", 4), ("run", 1), ("vs", 1, 0), ("vs", 1, 1), ("vs", 2, 0), ("r2", 0, 0),
    ("vs", 2, 1), ("vs", 0, 0), ("r2", 1, 1), ("vs", 0, 1), ("r2", 0, 1), ("r2", 1, 0),
    ("vz", 1, 0), ("vz", 1, 1), ("vz", 2, 0), ("vz", 2, 1), ("fin", 0), ("fin", 1), ("iout",),
    ("uout",),
)
QU, QV = 2, 2


def valid_gather(d, s, p):
    return s <= 2 or (s == 3 and p == d)


def column(row):
    n = row.shape[1]
    a = lax.broadcasted_iota(jnp.int32, (n, n), 0)
    b = lax.broadcasted_iota(jnp.int32, (n, n), 1)
    return jnp.sum(jnp.where(a == b, jnp.broadcast_to(row, (n, n)), 0.0), axis=1, keepdims=True)


def kernel(
    ue_h, ie_h, ud_h, ideg_h, tv, rows_h, uo, io,
    X, U, T, TT, Q, S, PS, R, SB, RB, ZS, ZB, ZR, VS, VR, US, UR, keys, plan, ue, ie, ud, ideg, uov, iov, order, rows,
    isem, osem, wsem, send, xz, xy, xs, uz, ux, ps, ry, rz, v0, vz,
):
    b = lax.axis_index("blk")
    g = lax.axis_index("grp")
    core = b % 2
    y = (b // 2) % NY
    zl = b // (2 * NY)
    x = g % NX
    zh = g // NX
    other = 1 - core

    def blk(z_, y_, c_):
        return {"blk": (z_ * NY + y_) * NC + c_}

    def grp(h_, x_):
        return {"grp": h_ * NX + x_}

    sib = blk(zl, y, other)
    ydev = (blk(zl, (y + 1) % NY, core), blk(zl, (y + NY - 1) % NY, core))
    y2dev = (blk(zl, (y + 2) % NY, core), blk(zl, (y + NY - 2) % NY, core))
    zrel = (zl, zl + 1 - 2 * (zl % 2), (zl + 2) % NZ, NZ - 1 - zl)
    zdev = tuple(blk(z_, y, core) for z_ in zrel)
    xrel = tuple((x + e) % NX for e in range(NX))
    xdev = tuple(grp(zh, x_) for x_ in xrel)
    hrel = (zh, (zh + NH - 1) % NH, (zh + 1) % NH)
    hdev = (None, grp(hrel[1], x), grp(hrel[2], x))
    pb0 = (zl // 2) * 2
    pb = (pb0, 2 - pb0)

    PART = TILE // QV
    bar = pltpu.get_barrier_semaphore()
    peers = (sib,) + ydev + y2dev + zdev[1:] + xdev[1:] + hdev[1:]
    for dev in peers:
        pl.semaphore_signal(bar, inc=1, device_id=dev, device_id_type=MESH)

    fetch = [
        pltpu.make_async_copy(a, v, isem.at[n])
        for n, (a, v) in enumerate(
            ((ideg_h, ideg), (ud_h, ud), (ie_h, ie), (ue_h, ue), (rows_h, rows), (tv, T))
        )
    ]
    for c in fetch:
        c.start()

    sends = []

    def put(src, dst, rsem, dev):
        c = pltpu.make_async_remote_copy(
            src_ref=src, dst_ref=dst, send_sem=send.at[len(sends)], recv_sem=rsem,
            device_id=dev, device_id_type=MESH,
        )
        c.start()
        sends.append(c)

    def got(dst, rsem, dev):
        pltpu.make_async_remote_copy(
            src_ref=dst, dst_ref=dst, send_sem=send.at[0], recv_sem=rsem,
            device_id=dev, device_id_type=MESH,
        ).wait_recv()

    for c in fetch[:4]:
        c.wait()
    iscale = column(lax.rsqrt(ideg[...].astype(F32)))
    uscale = column(lax.rsqrt(ud[...].astype(F32)))
    X[y * NZ + zl, core] = (ie[...] * iscale).astype(BF16)
    U[g] = (ue[...] * uscale).astype(BF16)
    U[ROWS] = jnp.zeros((TILE, D), BF16)

    pl.semaphore_wait(bar, len(peers))

    own = X.at[y * NZ + zl, core]
    for k in (1, 3, 2):
        put(own, own, xz.at[k - 1], zdev[k])
    def urows(j, x_, q):
        return U.at[hrel[j] * NX + x_, pl.ds(q * (TILE // QU), TILE // QU)]

    for q in range(QU):
        for j in (1, 2):
            put(urows(0, x, q), urows(0, x, q), uz.at[2 - j, q], hdev[j])
    for e in (2, 1, 3):
        put(U.at[g], U.at[g], ux.at[e - 1, 0, 0], xdev[e])

    def xreg(yy, p, c):
        return X.at[pl.ds(yy * NZ + pb[p], 2), c]

    def yfrom(d, s):
        return (y + NY - 1 - s) % NY if d == 0 else (y + 1 + s) % NY

    ocopy = pltpu.make_async_copy(plan, order, osem)

    def total(m, v):
        return jnp.sum(jnp.where(m, v, 0), axis=0, keepdims=True)

    def do_sort():
        fetch[4].wait()
        for i in range(NT):
            keys[i : i + 1, :] = jnp.full((1, 128), rows[i % SLOTS, i // SLOTS], jnp.int32)
        sub = lax.broadcasted_iota(jnp.int32, (NT, 128), 0)
        lane = lax.broadcasted_iota(jnp.int32, (NT, 128), 1)
        late = (sub // SLOTS) % NY == (y + 4) % NY
        kc = keys[...]
        kl = jnp.where(late, kc + 16, kc)
        uc = kl * NT + sub
        ur = jnp.sum(jnp.where(sub == lane, uc, 0), axis=0, keepdims=True)
        ur = jnp.where(lax.broadcasted_iota(jnp.int32, (1, 128), 1) < NT, ur, 1 << 20)
        rank = jnp.sum(jnp.where(ur < uc, 1, 0), axis=1, keepdims=True)
        hit = rank == lane

        plan[...] = jnp.zeros((8, 128), jnp.int32)
        plan[0:1, :] = total(hit, sub)
        plan[1:2, :] = total(hit, kl)
        plan[2:3, :] = jnp.where(total(kl == lane, 1) > 0, total(kl <= lane, 1), 0)
        plan[3:4, :] = jnp.where(total(kl == lane + 16, 1) > 0, total(kl <= lane + 16, 1), 0)
        ocopy.start()

    def xfirst(p):
        for d in (0, 1):
            put(xreg(y, p, core), xreg(y, p, core), xy.at[d, 0, p], ydev[d])

    def zgot(k):
        r = X.at[y * NZ + zrel[k], core]
        got(r, xz.at[k - 1], zdev[k])

    def flip(c, _):
        TT[c, :, 0:TILE] = T[2 * c].T
        TT[c, :, TILE:] = T[2 * c + 1].T
        return 0

    def flips(lo, hi):
        lax.fori_loop(lo, hi, flip, 0, unroll=2)

    def products(yy):
        def one(z_, _):
            c = z_ * NY + yy
            lhs = T[pl.ds(2 * c, 2)].reshape(SLOTS * TILE, TILE)
            out = jnp.dot(lhs, X[yy * NZ + z_].reshape(TILE, D), preferred_element_type=F32)
            Q[pl.ds(2 * c, 2)] = out.reshape(SLOTS, TILE, D)
            return 0

        lax.fori_loop(0, NZ, one, 0, unroll=4)

    def do_part(i):
        yd = (y + NY + GROUPS[i]) % NY
        if i == 0:
            for e in (1, 2, 3):
                got(U.at[hrel[0] * NX + xrel[e]], ux.at[3 - e, 0, 0], xdev[e])
                for j in (1, 2):
                    for q in range(QU):
                        got(urows(j, xrel[e], q), ux.at[3 - e, j, q], xdev[e])

        def one(z_, _):
            c = z_ * NY + yd
            rhs = jnp.concatenate([U[rows[0, c]], U[rows[1, c]]], axis=0)
            out = jnp.dot(TT[c], rhs, preferred_element_type=F32)
            PS[yd * NZ + z_] = out.reshape(NC, HALF, D)
            return 0

        lax.fori_loop(0, NZ, one, 0, unroll=4)
        put(PS.at[pl.ds(yd * NZ, NZ), other], R.at[pl.ds(yd * NZ, NZ)], ps.at[i], sib)

    have = set()

    def both(n, d, p):
        i = GROUPS.index(n if d == 0 or n == 4 else -n)
        yd = (y + NY + GROUPS[i]) % NY
        if i not in have:
            have.add(i)
            got(R.at[pl.ds(yd * NZ, NZ)], ps.at[i], sib)
        q = pl.ds(yd * NZ + pb[p], 2)
        return PS[q, core] + R[q]

    def pass_on(val, d, n, dev):
        SB[d, n] = val.astype(BF16)
        put(SB.at[d, n], RB.at[d, n], ry.at[d, n], dev)

    def came(d, n):
        got(RB.at[d, n], ry.at[d, n], ydev[1 - d])
        return RB[d, n].astype(F32)

    def do_r4(d):
        pass_on(both(4, d, d), d, 0, y2dev[d])

    def do_r3(d, p):
        pass_on(both(3, d, p), d, 1 + p, ydev[d])

    def do_r2(d, p):
        val = both(2, d, p) + came(d, 1 + p)
        if p == d:
            val = val + came(d, 0)
        pass_on(val, d, 3 + p, y2dev[d])

    def do_r1(d, p):
        pass_on(both(1, d, p), d, 5 + p, ydev[d])

    def do_fin(p):
        val = both(0, 0, p)
        for d in (0, 1):
            val = val + came(d, 3 + p) + came(d, 5 + p)
        ZS[pl.ds(pb[p], 2)] = val
        ZB[pl.ds(pb[p], 2)] = val.astype(BF16)
        for k in ((1,), (2, 3))[p]:
            put(ZB.at[zrel[k]], ZR.at[k - 1], rz.at[k - 1], zdev[k])

    S[0] = jnp.zeros((TILE, D), F32)

    def running(lo, hi):
        def one(k, acc):
            keep = jnp.where(order[1, k] == order[1, jnp.maximum(k - 1, 0)], 1.0, 0.0)
            acc = acc * keep + Q[order[0, k]]
            S[k + 1] = acc
            return acc

        lax.fori_loop(lo, hi, one, jnp.zeros((TILE, D), F32), unroll=2)

    def do_run(late):
        if late:
            running(NT - 2 * NZ, NT)
        else:
            ocopy.wait()
            running(0, NT - 2 * NZ)

    def user_sum(j, x_, q):
        r = hrel[j] * NX + x_
        w = pl.ds(q * PART, PART)
        return S[order[2, r], w] + S[order[3, r], w]

    def do_zf(p):
        for k in ((1,), (3, 2))[p]:
            zgot(k)
        xfirst(p)
        if p == 1:
            r = X.at[pl.ds(y * NZ, NZ), core]
            put(r, r, xs.at[0, 4, 0], sib)

    def do_flip(i):
        if i == 0:
            fetch[5].wait()
        flips(i * COLS // 4, (i + 1) * COLS // 4)

    def do_ip(d, s, p):
        r = xreg(yfrom(d, s), p, core)
        got(r, xy.at[d, s, p], ydev[1 - d])
        if valid_gather(d, s + 1, p):
            put(r, r, xy.at[d, s + 1, p], ydev[d])
        put(r, r, xs.at[d, s, p], sib)

    def do_uz(j, q):
        r = urows(j, x, q)
        got(r, uz.at[j - 1, q], hdev[j])
        for e in (2, 1, 3):
            put(r, r, ux.at[e - 1, j, q], xdev[e])

    def do_prod(off):
        if off == 0:
            r = X.at[pl.ds(y * NZ, NZ), other]
            got(r, xs.at[0, 4, 0], sib)
        else:
            s = abs(off) - 1
            for d in (0, 1):
                for p in (0, 1):
                    if off == 4 and p == d or off != 4 and d == (off > 0):
                        got(xreg(yfrom(d, s), p, other), xs.at[d, s, p], sib)
        products((y + NY + off) % NY)

    def do_vs(j, q):
        w = pl.ds(q * PART, PART)
        for e in (2, 1, 3):
            VS[e - 1, j, w] = user_sum(j, xrel[e], q).astype(BF16)
            put(VS.at[e - 1, j, w], VR.at[e - 1, j, w], v0.at[e - 1, j, q], xdev[e])

    def user_total(j, q):
        w = pl.ds(q * PART, PART)
        t = user_sum(j, x, q)
        for e in (1, 2, 3):
            got(VR.at[e - 1, j, w], v0.at[e - 1, j, q], xdev[NX - e])
            t = t + VR[e - 1, j, w].astype(F32)
        return t

    def do_vz(j, q):
        w = pl.ds(q * PART, PART)
        US[j - 1, w] = user_total(j, q).astype(BF16)
        put(US.at[j - 1, w], UR.at[2 - j, w], vz.at[2 - j, q], hdev[j])

    out = [pltpu.make_async_copy(uov, uo, wsem.at[0]), pltpu.make_async_copy(iov, io, wsem.at[1])]

    def do_uout():
        for q in range(QV):
            w = slice(q * PART, (q + 1) * PART)
            t = user_total(0, q)
            for j in (1, 2):
                got(UR.at[j - 1, pl.ds(q * PART, PART)], vz.at[j - 1, q], hdev[j])
                t = t + UR[j - 1, w].astype(F32)
            uov[w] = 0.5 * (ue[w] + uscale[w] * t)
        out[0].start()

    def do_iout():
        acc = ZS[zl]
        for k in (1, 2, 3):
            got(ZR.at[k - 1], rz.at[k - 1], zdev[k])
            acc = acc + ZR[k - 1].astype(F32)
        iov[...] = 0.5 * (ie[...] + iscale * acc)
        out[1].start()

    steps = {
        "zf": do_zf, "sort": do_sort, "flip": do_flip, "ip": do_ip, "uz": do_uz, "part": do_part,
        "prod": do_prod, "run": do_run, "r4": do_r4, "r3": do_r3, "r2": do_r2, "r1": do_r1,
        "fin": do_fin, "vs": do_vs, "vz": do_vz, "uout": do_uout, "iout": do_iout,
    }
    for name, *at in ORDER:
        steps[name](*at)

    for c in out:
        c.wait()
    for c in sends:
        c.wait_send()


def hand_over(a, b, c, d, va, vb, sem):
    in_a = pltpu.make_async_copy(a, va, sem.at[0])
    in_b = pltpu.make_async_copy(b, vb, sem.at[1])
    out_a = pltpu.make_async_copy(va, c, sem.at[2])
    out_b = pltpu.make_async_copy(vb, d, sem.at[3])
    in_a.start()
    in_b.start()
    in_a.wait()
    out_a.start()
    in_b.wait()
    out_b.start()
    out_a.wait()
    out_b.wait()


def on_device(user_embed, item_embed, user_degree, item_degree, tile_values, tile_rows):
    hbm = pl.BlockSpec(memory_space=pltpu.HBM)
    dma = pltpu.SemaphoreType.DMA
    shapes = (
        jax.ShapeDtypeStruct((TILE, D), F32),
        jax.ShapeDtypeStruct((HALF, D), F32),
    )
    user_out, item_out = pl.pallas_call(
        kernel,
        out_shape=shapes,
        in_specs=[hbm] * 6,
        out_specs=(hbm, hbm),
        scratch_shapes=[
            pltpu.VMEM((COLS, NC, HALF, D), BF16),
            pltpu.VMEM((ROWS + 1, TILE, D), BF16),
            pltpu.VMEM((NT, TILE, TILE), BF16),
            pltpu.VMEM((COLS, TILE, SLOTS * TILE), BF16),
            pltpu.VMEM((NT, TILE, D), F32),
            pltpu.VMEM((NT + 1, TILE, D), F32),
            pltpu.VMEM((COLS, NC, HALF, D), F32),
            pltpu.VMEM((COLS, HALF, D), F32),
            pltpu.VMEM((2, 7, 2, HALF, D), BF16),
            pltpu.VMEM((2, 7, 2, HALF, D), BF16),
            pltpu.VMEM((NZ, HALF, D), F32),
            pltpu.VMEM((NZ, HALF, D), BF16),
            pltpu.VMEM((NZ - 1, HALF, D), BF16),
            pltpu.VMEM((NX - 1, NH, TILE, D), BF16),
            pltpu.VMEM((NX - 1, NH, TILE, D), BF16),
            pltpu.VMEM((2, TILE, D), BF16),
            pltpu.VMEM((2, TILE, D), BF16),
            pltpu.VMEM((NT, 128), jnp.int32),
            pltpu.VMEM((8, 128), jnp.int32),
            pltpu.VMEM((TILE, D), F32),
            pltpu.VMEM((HALF, D), F32),
            pltpu.VMEM((1, TILE), jnp.int32),
            pltpu.VMEM((1, HALF), jnp.int32),
            pltpu.VMEM((TILE, D), F32),
            pltpu.VMEM((HALF, D), F32),
            pltpu.SMEM((8, 128), jnp.int32),
            pltpu.SMEM((SLOTS, COLS), jnp.int32),
            dma((6,)),
            dma(()),
            dma((2,)),
            dma((104,)),
            dma((3,)),
            dma((2, 4, 2)),
            dma((2, 5, 2)),
            dma((2, 2)),
            dma((3, 3, 2)),
            dma((8,)),
            dma((2, 7)),
            dma((3,)),
            dma((3, 3, 2)),
            dma((2, 2)),
        ],
        compiler_params=pltpu.CompilerParams(
            collective_id=0, has_side_effects=True, vmem_limit_bytes=62 << 20
        ),
    )(
        user_embed,
        item_embed[0],
        user_degree.reshape(1, TILE),
        item_degree,
        tile_values.reshape(NT, TILE, TILE),
        tile_rows.T,
    )
    user_out, item_out = pl.pallas_call(
        hand_over,
        out_shape=shapes,
        in_specs=[hbm] * 2,
        out_specs=(hbm, hbm),
        scratch_shapes=[pltpu.VMEM((TILE, D), F32), pltpu.VMEM((HALF, D), F32), dma((4,))],
        compiler_params=pltpu.CompilerParams(vmem_limit_bytes=62 << 20),
    )(user_out, item_out)
    return user_out, item_out[None]


def solution(mesh):
    return jax.shard_map(
        on_device,
        mesh=mesh,
        in_specs=(
            P(("blk", "grp"), None),
            P("grp", "blk", None),
            P(("blk", "grp")),
            P("grp", "blk"),
            P("blk", "grp", None, None),
            P("blk", "grp"),
        ),
        out_specs=(P(("blk", "grp"), None), P("grp", "blk", None)),
        check_vma=False,
    )
```
